256 devices in a mesh: cent: 128 (over z, x, y), rows: 2 (over core).
Axes of the slice: x: 4, y: 4, z: 8, core: 2. Of those that a mesh axis runs over, the one named last changes fastest.
Arguments:
- codebook: float32 [131072, 768], P('cent'), may hold values from -6 to 6
- batch: bfloat16 [2, 2, 1024, 768], P(None, 'rows', 'cent'), may hold values from -7 to 7
- dead_ids: int32 [2, 128], replicated, may hold values from 0 to 131071, as said below
- reseed_rows: int32 [2, 128], replicated, may hold values from 0 to 1023
- source_group: int32 [2, 128], replicated, may hold values from 0 to 1
Outputs:
- new_codebook: float32 [131072, 768], P('cent')
- energy: float32 [2, 2, 1024], P(None, 'rows', 'cent')
The draws below stay inside these ranges and needn't reach their ends.
Inputs may be any that keep to these rules, and one draw needn't show every extreme that they name: `dead_ids`: in each iteration the 128 ids are distinct, one in each of 128 equal consecutive ranges of centroid ids, in random order.
All inputs are finite; a program needn't handle non-finite values.
Results may differ from the reference program's by a relative error of at most 0.0055.
Values may be sent and summed in bfloat16 or wider, within the bound.
A program may use at most 128 MiB of HBM per device.

```python
import math
import jax
import jax.numpy as jnp
from jax import lax

D = 768
ITERS = 2
NDEAD = 128
K = 131072
GROUP_ROWS = 1024
GROUPS = 2


def base_codebook(key):
    table = jax.random.normal(jax.random.fold_in(key, 11), (K, D), jnp.float32)
    stride = K // 32
    index = jnp.arange(K)
    table = jnp.where((index % stride == 0)[:, None], table * 2.2, table)
    noise = jax.random.normal(jax.random.fold_in(key, 12), (K, D), jnp.float32) * (0.4 ** 0.5 * D ** (-0.25))
    shifted = jnp.roll(table, 1, axis=0)
    table = jnp.where((index % stride == 1)[:, None], shifted + noise, table)
    return jnp.clip(table, -6.0, 6.0)


def draw_codebook(key, part):
    return base_codebook(key)


def draw_batch(key, part):
    table = base_codebook(key)
    key = jax.random.fold_in(key, 2)
    shape = (ITERS, GROUPS, GROUP_ROWS, D)
    values = jnp.clip(jax.random.normal(key, shape, jnp.float32), -6.0, 6.0)
    stride = K // 32
    iters_index = jnp.arange(ITERS)[:, None, None]
    group_index = jnp.arange(GROUPS)[None, :, None]
    row_index = jnp.arange(GROUP_ROWS)[None, None, :]
    chosen = jnp.broadcast_to((row_index // 32 + 7 * group_index + 13 * iters_index) * stride % K, shape[:3])
    strength = jnp.broadcast_to(0.6 + 0.2 * (row_index // 32 % 3).astype(jnp.float32), shape[:3])
    planted = table[chosen] * strength[..., None]
    planted_mask = jnp.broadcast_to(row_index % 32 == 0, shape[:3])
    return jnp.where(planted_mask[..., None], planted, values).astype(jnp.bfloat16)


def shuffle_one(shuffle_key):
    return jax.random.permutation(shuffle_key, NDEAD)


def draw_dead_ids(key, part):
    key = jax.random.fold_in(key, 3)
    span = K // NDEAD
    offsets = jax.random.randint(key, (ITERS, NDEAD), 0, span)
    offsets = offsets.at[:, 0].set(0).at[:, NDEAD - 1].set(span - 1)
    ids_sorted = jnp.arange(NDEAD, dtype=jnp.int32)[None, :] * span + offsets
    orders = jax.vmap(shuffle_one)(jax.random.split(jax.random.fold_in(key, 4), ITERS))
    return jnp.take_along_axis(ids_sorted, orders, axis=1).astype(jnp.int32)


def plant(values, key, least, top_value):
    extent = values.shape
    spot = [jax.random.randint(jax.random.fold_in(key, axis), (), 0, extent[axis]) for axis in range(len(extent))]
    values = values.at[tuple(spot)].set(least)
    longest = extent.index(max(extent))
    spot[longest] = (spot[longest] + 1) % extent[longest]
    return values.at[tuple(spot)].set(top_value)


def setup_inputs(seed: int = 0) -> dict:
    key_of = jax.random.split(jax.random.key(seed), 6)
    return {
        "codebook": draw_codebook(jax.random.fold_in(key_of[5], 71), 0),
        "batch": draw_batch(jax.random.fold_in(key_of[5], 71), 0),
        "dead_ids": draw_dead_ids(jax.random.fold_in(key_of[5], 71), 0),
        "reseed_rows": plant(jax.random.randint(key_of[3], (ITERS, NDEAD), 0, GROUP_ROWS), jax.random.fold_in(key_of[3], 1), 0, GROUP_ROWS - 1).astype(jnp.int32),
        "source_group": plant(jax.random.randint(key_of[4], (ITERS, NDEAD), 0, GROUPS), jax.random.fold_in(key_of[4], 1), 0, GROUPS - 1).astype(jnp.int32),
    }


def soft_update(table, current, sharpness):
    halved = table.astype(jnp.bfloat16)
    squares = lax.optimization_barrier(jnp.sum(table * table, axis=1))
    width = math.gcd(current.shape[0], 128)
    blocks = current.reshape(-1, width, D)

    def visit(running, row_block):
        cent_sums, counts = running
        scores = sharpness * (2.0 * jnp.dot(row_block, halved.T, preferred_element_type=jnp.float32) - squares[None, :])
        row_top = lax.optimization_barrier(jnp.max(scores, axis=1))
        row_total = lax.optimization_barrier(jnp.sum(jnp.exp(scores - row_top[:, None]), axis=1))
        weights = (jnp.exp(scores - row_top[:, None]) / row_total[:, None]).astype(jnp.bfloat16)
        cent_sums = cent_sums + jnp.dot(weights.T, row_block, preferred_element_type=jnp.float32)
        counts = counts + lax.optimization_barrier(jnp.sum(weights.astype(jnp.float32), axis=0))
        return ((cent_sums, counts), (row_top + jnp.log(row_total)) / (sharpness * D))
    start_state = (jnp.zeros(table.shape, jnp.float32), jnp.zeros((table.shape[0],), jnp.float32))
    (cent_sums, counts), energies = lax.scan(visit, start_state, blocks)
    updated = table + (cent_sums - counts[:, None] * table) / (counts[:, None] + 0.05)
    return (updated, energies.reshape(-1))

def reference(codebook, batch, dead_ids, reseed_rows, source_group):
    sharpness = 5.0 / math.sqrt(D)
    table = codebook
    results = []
    for iteration in range(ITERS):
        current = batch[iteration].reshape(GROUPS * GROUP_ROWS, D)
        table, energies = soft_update(table, current, sharpness)
        results.append(energies.reshape(GROUPS, GROUP_ROWS))
        picked = batch[iteration][source_group[iteration].astype(jnp.int32), reseed_rows[iteration].astype(jnp.int32)]
        table = table.at[dead_ids[iteration].astype(jnp.int32)].set(picked.astype(jnp.float32))
    return (table, jnp.stack(results))
```

```python
import math

import jax
import jax.numpy as jnp
from jax import lax
from jax.experimental import pallas as pl
from jax.experimental.pallas import tpu as pltpu
from jax.sharding import PartitionSpec as P

D = 768
ITERS = 2
NZ, NX, NY = 8, 4, 4
NS = 4
HALF = D // 2
SHARP = 5.0 / math.sqrt(D)
LOG2E = 1.0 / math.log(2.0)
MESH = pl.DeviceIdType.MESH
LANES = 128


def wrap(value, size):
    return lax.rem(value + size, size)


def kernel(
    book,
    batch,
    dead,
    reseed,
    source,
    out,
    energy,
    xb0,
    xb1,
    own16,
    pair16,
    tab,
    cb16,
    qb,
    ebuf,
    wbuf,
    mbuf,
    lbuf,
    fbuf,
    st1,
    st2,
    load_sem,
    pair_sem,
    z_sem,
    s_sem,
    t_sem,
    p_sem,
    a_sem,
    b_sem,
    o_sem,
):
    cent = lax.axis_index("cent")
    g = lax.axis_index("rows")
    z = lax.div(cent, NX * NY)
    x = lax.rem(lax.div(cent, NY), NX)
    y = lax.rem(cent, NY)
    xbs = (xb0, xb1)
    count = tab.shape[0]
    first = g * count
    cols = pl.ds(pl.multiple_of(g * HALF, LANES), HALF)
    their_cols = pl.ds(pl.multiple_of((1 - g) * HALF, LANES), HALF)

    def device(zz, xx, yy, gg):
        return (zz * (NX * NY) + xx * NY + yy, gg)

    def line(d2, d3, core):
        dx = jnp.where(core == 0, d2, d3)
        dy = jnp.where(core == 0, d3, d2)
        return wrap(x + dx, NX), wrap(y + dy, NY)

    partner = device(z, x, y, 1 - g)

    load = pltpu.make_async_copy(book.at[pl.ds(pl.multiple_of(first, 256), count)], tab, load_sem)
    load.start()

    barrier = pltpu.get_barrier_semaphore()
    for d in range(1, NZ):
        pl.semaphore_signal(barrier, inc=1, device_id=device(wrap(z + d, NZ), x, y, g), device_id_type=MESH)
    for d in range(1, NS):
        pl.semaphore_signal(barrier, inc=1, device_id=device(z, wrap(x + d, NX), y, g), device_id_type=MESH)
        pl.semaphore_signal(barrier, inc=1, device_id=device(z, x, wrap(y + d, NY), g), device_id_type=MESH)
    pl.semaphore_signal(barrier, inc=1, device_id=partner, device_id_type=MESH)
    own16[...] = jnp.concatenate(
        [batch[0, 0].astype(jnp.float32), batch[1, 0].astype(jnp.float32)], axis=0
    ).astype(jnp.bfloat16)
    pl.semaphore_wait(barrier, NZ - 1 + 2 * (NS - 1) + 1)

    swap = pltpu.make_async_remote_copy(
        src_ref=own16.at[:, their_cols],
        dst_ref=pair16,
        send_sem=pair_sem.at[0],
        recv_sem=pair_sem.at[1],
        device_id=partner,
        device_id_type=MESH,
    )
    swap.start()
    swap.wait()
    mine = own16[:, cols].astype(jnp.float32)
    theirs = pair16[...].astype(jnp.float32)
    for i in range(ITERS):
        rows_i = slice(8 * i, 8 * i + 8)
        a = jnp.where(g == 0, mine[rows_i], theirs[rows_i])
        b = jnp.where(g == 0, theirs[rows_i], mine[rows_i])
        xbs[i][z, x, y, :, cols] = jnp.concatenate([a, b], axis=0).astype(jnp.bfloat16)

    def z_copy(i, d, zz):
        ref = xbs[i].at[zz, x, y, :, cols]
        return pltpu.make_async_remote_copy(
            src_ref=ref,
            dst_ref=ref,
            send_sem=z_sem.at[0, i, d],
            recv_sem=z_sem.at[1, i, d],
            device_id=device(wrap(z + d, NZ), x, y, g),
            device_id_type=MESH,
        )

    def line_copy(i, d2, d3, core, sems, k, to):
        xx, yy = line(-d2, -d3, core)
        where = cols if core is g else their_cols
        ref = xbs[i].at[:, xx, yy, :, where]
        return pltpu.make_async_remote_copy(
            src_ref=ref,
            dst_ref=ref,
            send_sem=sems.at[0, i, k],
            recv_sem=sems.at[1, i, k],
            device_id=to,
            device_id_type=MESH,
        )

    def second(i, d, d2=0):
        xx, yy = line(d, 0, g)
        return line_copy(i, d2, 0, g, s_sem, d, device(z, xx, yy, g))

    def third(i, d, d2, back=0):
        xx, yy = line(0, d, g)
        return line_copy(i, d2, back, g, t_sem, d * NS + d2, device(z, xx, yy, g))

    def across(i, d2, d3, core):
        return line_copy(i, d2, d3, core, p_sem, d3 * NS + d2, partner)

    def send_z(i):
        for d in range(1, NZ):
            z_copy(i, d, z).start()

    def wait_z(i):
        for d in range(1, NZ):
            z_copy(i, d, wrap(z - d, NZ)).wait_recv()

    def send_own_line(i):
        for d in range(1, NS):
            second(i, d).start()
        for d in range(1, NS):
            third(i, d, 0).start()
        across(i, 0, 0, g).start()

    def pass_second(i):
        for d2 in range(1, NS):
            second(i, d2, d2).wait_recv()
            for d in range(1, NS):
                third(i, d, d2).start()
            across(i, d2, 0, g).start()

    def pass_third(i):
        for d2 in range(NS):
            for d3 in range(1, NS):
                third(i, d3, d2, d3).wait_recv()
                across(i, d2, d3, g).start()

    def wait_across(i):
        for d3 in range(NS):
            for d2 in range(NS):
                across(i, d2, d3, 1 - g).wait_recv()

    def finish_sends(i):
        for d in range(1, NZ):
            z_copy(i, d, z).wait_send()
        for d in range(1, NS):
            second(i, d).wait_send()
            for d2 in range(NS):
                third(i, d, d2).wait_send()
        for d3 in range(NS):
            for d2 in range(NS):
                across(i, d2, d3, g).wait_send()

    def prepare():
        for k in range(count // LANES):
            rows_k = slice(k * LANES, (k + 1) * LANES)
            table = tab[rows_k, :]
            cb16[rows_k, :] = table.astype(jnp.bfloat16)
            q = jnp.sum(table * table, axis=1, keepdims=True) * (SHARP * LOG2E)
            qb[rows_k, :] = jnp.broadcast_to(q, (LANES, LANES))

    def scores(i):
        @pl.loop(0, NZ)
        def _(t):
            tile = xbs[i][t].reshape(NX * NY * 16, D)
            acc = lax.dot_general(
                cb16[...], tile, (((1,), (1,)), ((), ())), preferred_element_type=jnp.float32
            )
            for h in range(2):
                s = acc[:, h * LANES : (h + 1) * LANES] * (2.0 * SHARP * LOG2E) - qb[...]
                top = jnp.max(s, axis=0, keepdims=True)
                e = jnp.exp2(s - top)
                total = jnp.sum(e, axis=0, keepdims=True)
                ebuf[2 * t + h] = e
                mbuf[pl.ds(2 * t + h, 1), :] = top
                lbuf[pl.ds(2 * t + h, 1), :] = top + jnp.log2(total)

    def merge(parts):
        top = parts[0]
        for part in parts[1:]:
            top = jnp.maximum(top, part)
        total = jnp.exp2(parts[0] - top)
        for part in parts[1:]:
            total = total + jnp.exp2(part - top)
        return top + jnp.log2(total)

    def stat_one(i, d, h, zz):
        gg = jnp.where(h == 0, g, 1 - g)
        return pltpu.make_async_remote_copy(
            src_ref=lbuf.at[pl.ds(pl.multiple_of(gg * 8, 8), 8)],
            dst_ref=st1.at[i, d, h],
            send_sem=a_sem.at[0, i, d, h],
            recv_sem=a_sem.at[1, i, d, h],
            device_id=device(zz, x, y, gg),
            device_id_type=MESH,
        )

    def stat_two(i, dx, dy, h):
        gg = jnp.where(h == 0, g, 1 - g)
        return pltpu.make_async_remote_copy(
            src_ref=st1.at[i, 0, 0],
            dst_ref=st2.at[i, dx, dy, h],
            send_sem=b_sem.at[0, i, dx, dy, h],
            recv_sem=b_sem.at[1, i, dx, dy, h],
            device_id=device(z, wrap(x + dx, NX), wrap(y + dy, NY), gg),
            device_id_type=MESH,
        )

    def peers_one():
        return [(d, h) for d in (4, 3, 5, 2, 6, 1, 7, 0) for h in range(2) if d or h]

    def peers_two():
        order = sorted(
            [(dx, dy) for dx in range(NX) for dy in range(NY)],
            key=lambda v: -(min(v[0], NX - v[0]) + min(v[1], NY - v[1])),
        )
        return [(dx, dy, h) for dx, dy in order for h in range(2) if dx or dy or h]

    def reduce_stats(i, between):
        for d, h in peers_one():
            stat_one(i, d, h, wrap(z + d, NZ)).start()
        for d, h in peers_one():
            stat_one(i, d, h, wrap(z + d, NZ)).wait_recv()
        parts = [lbuf[pl.ds(pl.multiple_of(g * 8, 8), 8), :]]
        parts += [st1[i, d, h] for d, h in peers_one()]
        st1[i, 0, 0] = merge(parts)
        for dx, dy, h in peers_two():
            stat_two(i, dx, dy, h).start()
        between()
        for dx, dy, h in peers_two():
            stat_two(i, dx, dy, h).wait_recv()
        same = merge([st1[i, 0, 0]] + [st2[i, dx, dy, 0] for dx, dy, h in peers_two() if h == 0])
        other = merge([st2[i, dx, dy, 1] for dx, dy, h in peers_two() if h == 1])
        low = jnp.where(g == 0, same, other)
        high = jnp.where(g == 0, other, same)
        return jnp.concatenate([low, high], axis=0)

    def finish_stats(i):
        for d, h in peers_one():
            stat_one(i, d, h, wrap(z + d, NZ)).wait_send()
        for dx, dy, h in peers_two():
            stat_two(i, dx, dy, h).wait_send()

    def reseeding(i):
        def look(j, carry):
            place, row = carry
            here = dead[i, j] - cent * (2 * count)
            inside = (here >= 0) & (here < 2 * count)
            place = place + jnp.where(inside, here, 0)
            row = row + jnp.where(inside, source[i, j] * 1024 + reseed[i, j], 0)
            return place, row

        place, row = lax.fori_loop(0, dead.shape[1], look, (jnp.int32(0), jnp.int32(0)))
        group = lax.div(row, 1024)
        inner = lax.rem(row, 1024)
        return place - first, group, inner

    def picked_row(i, group, inner):
        c = lax.div(inner, 8)
        block = xbs[i][lax.div(c, NX * NY), lax.rem(lax.div(c, NY), NX), lax.rem(c, NY)]
        which = lax.broadcasted_iota(jnp.int32, (16, D), 0) == group * 8 + lax.rem(inner, 8)
        return jnp.sum(jnp.where(which, block.astype(jnp.float32), 0.0), axis=0, keepdims=True)

    def update(i, final, picked, place):
        fbuf[...] = jnp.exp2(mbuf[...] - final)
        xall = xbs[i].reshape(NZ * NX * NY * 16, D)
        step = 256
        for k in range(count // step):
            rows_k = slice(k * step, (k + 1) * step)
            tally = jnp.zeros((step, LANES), jnp.float32)
            for t in range(2 * NZ):
                w = (ebuf[t, rows_k, :] * fbuf[t : t + 1, :]).astype(jnp.bfloat16)
                wbuf[rows_k, t * LANES : (t + 1) * LANES] = w
                tally = tally + w.astype(jnp.float32)
            counts = jnp.sum(tally, axis=1, keepdims=True)
            sums = jnp.dot(wbuf[rows_k, :], xall[...], preferred_element_type=jnp.float32)
            table = tab[rows_k, :]
            table = table + (sums - counts * table) * (1.0 / (counts + 0.05))
            rows = lax.broadcasted_iota(jnp.int32, (step, D), 0) + k * step
            tab[rows_k, :] = jnp.where(rows == place, picked, table)

    def write_energy(i, final):
        lbuf[...] = final
        offset = (x * NY + y) * 16 + g * 8
        row = lbuf[pl.ds(2 * z + lax.div(offset, LANES), 1), :]
        row = pltpu.roll(row, wrap(-lax.rem(offset, LANES), LANES), 1)
        energy[i] = row[:, :8] * (1.0 / (LOG2E * SHARP * D))

    send_z(0)
    send_z(1)
    place0, group0, inner0 = reseeding(0)
    place1, group1, inner1 = reseeding(1)
    wait_z(0)
    send_own_line(0)
    load.wait()
    prepare()
    pass_second(0)
    pass_third(0)
    wait_z(1)
    wait_across(0)

    send_own_line(1)
    scores(0)
    final = reduce_stats(0, lambda: pass_second(1))
    finish_stats(0)
    write_energy(0, final)
    update(0, final, picked_row(0, group0, inner0), place0)
    prepare()
    pass_third(1)
    wait_across(1)

    scores(1)
    final = reduce_stats(1, lambda: None)
    finish_stats(1)
    write_energy(1, final)
    update(1, final, picked_row(1, group1, inner1), place1)

    part = out.at[pl.ds(pl.multiple_of(first, 256), count)]
    keep = pltpu.make_async_copy(tab, part, load_sem)
    keep.start()
    give = pltpu.make_async_remote_copy(
        src_ref=tab,
        dst_ref=part,
        send_sem=o_sem.at[0],
        recv_sem=o_sem.at[1],
        device_id=partner,
        device_id_type=MESH,
    )
    give.start()
    finish_sends(0)
    finish_sends(1)
    keep.wait()
    give.wait()


def shards(codebook, batch, dead_ids, reseed_rows, source_group):
    held = codebook.shape[0]
    count = held // 2
    vmem = pl.BlockSpec(memory_space=pltpu.VMEM)
    smem = pl.BlockSpec(memory_space=pltpu.SMEM)
    anywhere = pl.BlockSpec(memory_space=pl.ANY)
    rows = NZ * NX * NY * 16
    dma = pltpu.SemaphoreType.DMA
    table, energies = pl.pallas_call(
        kernel,
        out_shape=(
            jax.ShapeDtypeStruct((held, D), jnp.float32),
            jax.ShapeDtypeStruct((ITERS, 1, 8), jnp.float32),
        ),
        in_specs=[anywhere, vmem, smem, smem, smem],
        out_specs=(anywhere, vmem),
        scratch_shapes=[
            pltpu.VMEM((NZ, NX, NY, 16, D), jnp.bfloat16),
            pltpu.VMEM((NZ, NX, NY, 16, D), jnp.bfloat16),
            pltpu.VMEM((16, D), jnp.bfloat16),
            pltpu.VMEM((16, HALF), jnp.bfloat16),
            pltpu.VMEM((count, D), jnp.float32),
            pltpu.VMEM((count, D), jnp.bfloat16),
            pltpu.VMEM((count, LANES), jnp.float32),
            pltpu.VMEM((2 * NZ, count, LANES), jnp.float32),
            pltpu.VMEM((count, rows), jnp.bfloat16),
            pltpu.VMEM((2 * NZ, LANES), jnp.float32),
            pltpu.VMEM((2 * NZ, LANES), jnp.float32),
            pltpu.VMEM((2 * NZ, LANES), jnp.float32),
            pltpu.VMEM((ITERS, NZ, 2, 8, LANES), jnp.float32),
            pltpu.VMEM((ITERS, NX, NY, 2, 8, LANES), jnp.float32),
            dma,
            dma((2,)),
            dma((2, ITERS, NZ)),
            dma((2, ITERS, NS)),
            dma((2, ITERS, NS * NS)),
            dma((2, ITERS, NS * NS)),
            dma((2, ITERS, NZ, 2)),
            dma((2, ITERS, NX, NY, 2)),
            dma((2,)),
        ],
        compiler_params=pltpu.CompilerParams(
            collective_id=0, has_side_effects=True, vmem_limit_bytes=48 * 2**20
        ),
        name="soft_kmeans",
    )(codebook, batch, dead_ids, reseed_rows, source_group)
    return (table, energies)


def solution(mesh):
    return jax.shard_map(
        shards,
        mesh=mesh,
        in_specs=(P("cent", None), P(None, "rows", "cent", None), P(), P(), P()),
        out_specs=(P("cent", None), P(None, "rows", "cent")),
        check_vma=False,
    )
```

```python
import math

import jax
import jax.numpy as jnp
from jax import lax
from jax.experimental import pallas as pl
from jax.experimental.pallas import tpu as pltpu
from jax.sharding import PartitionSpec as P

D = 768
ITERS = 2
NZ, NX, NY = 8, 4, 4
NS = 4
HALF = D // 2
SHARP = 5.0 / math.sqrt(D)
LOG2E = 1.0 / math.log(2.0)
MESH = pl.DeviceIdType.MESH
LANES = 128
PARTS = ((0, 256), (256, 256))
ORDER = (0, 1, 7, 2, 6, 3, 5, 4)
LAG3, LAGP = 3, 2


def wrap(value, size):
    return lax.rem(value + size, size)


def kernel(
    book,
    batch_in,
    ids_in,
    out,
    energy,
    xb0,
    xb1,
    batch,
    ids,
    own16,
    first,
    tab,
    cb16,
    qb,
    sb0,
    sb1,
    ebuf,
    wbuf,
    sums,
    tally,
    mbuf,
    lbuf,
    fin,
    merged,
    st1,
    st2,
    load_sem,
    f_sem,
    z_sem,
    t_sem,
    p_sem,
    a_sem,
    b_sem,
    o_sem,
):
    cent = lax.axis_index("cent")
    g = lax.axis_index("rows")
    z = lax.div(cent, NX * NY)
    x = lax.rem(lax.div(cent, NY), NX)
    y = lax.rem(cent, NY)
    xbs = (xb0, xb1)
    sbs = (sb0, sb1)
    count = tab.shape[0]
    base = g * count

    def half(core):
        return pl.ds(pl.multiple_of(core * HALF, LANES), HALF)

    def device(zz, xx, yy, gg):
        return (zz * (NX * NY) + xx * NY + yy, gg)

    def along(core, d):
        return wrap(x + (1 - core) * d, NX), wrap(y + core * d, NY)

    partner = device(z, x, y, 1 - g)

    loads = [
        pltpu.make_async_copy(batch_in, batch, load_sem.at[0]),
        pltpu.make_async_copy(ids_in, ids, load_sem.at[1]),
        pltpu.make_async_copy(
            book.at[pl.ds(pl.multiple_of(base, 256), count)], tab, load_sem.at[2]
        ),
    ]
    for load in loads:
        load.start()

    barrier = pltpu.get_barrier_semaphore()

    def greet(to):
        pl.semaphore_signal(barrier, inc=1, device_id=to, device_id_type=MESH)

    for d in (1, 2, NZ - 2, NZ - 1):
        greet(device(wrap(z + d, NZ), x, y, g))
    for d in range(1, NS):
        for gg in (g, 1 - g):
            greet(device(z, wrap(x + d, NX), y, gg))
            greet(device(z, x, wrap(y + d, NY), gg))
    greet(partner)
    loads[0].wait()
    own16[...] = jnp.concatenate(
        [batch[0, 0].astype(jnp.float32), batch[1, 0].astype(jnp.float32)], axis=0
    ).astype(jnp.bfloat16)
    pl.semaphore_wait(barrier, 4 + 4 * (NS - 1) + 1)

    def first_copy(d, h):
        core = g if h == 0 else 1 - g
        xx, yy = along(core, d)
        return pltpu.make_async_remote_copy(
            src_ref=own16.at[:, half(core)],
            dst_ref=first.at[d, h],
            send_sem=f_sem.at[0, d, h],
            recv_sem=f_sem.at[1, d, h],
            device_id=device(z, xx, yy, core),
            device_id_type=MESH,
        )

    firsts = [(d, h) for d in (2, 1, 3, 0) for h in range(2) if d or h]
    for d, h in firsts:
        first_copy(d, h).start()
    first[0, 0] = own16[:, half(g)]

    def place_line():
        for d, h in firsts:
            first_copy(d, h).wait_recv()
        for d in range(NS):
            same = first[d, 0].astype(jnp.float32)
            other = first[d, 1].astype(jnp.float32)
            xx, yy = along(g, -d)
            for i in range(ITERS):
                rows_i = slice(8 * i, 8 * i + 8)
                a = jnp.where(g == 0, same[rows_i], other[rows_i])
                b = jnp.where(g == 0, other[rows_i], same[rows_i])
                block = jnp.concatenate([a, b], axis=0).astype(jnp.bfloat16)
                xbs[i][z, xx, yy, :, half(g)] = block

    def by_core(f):
        pl.when(g == 0)(lambda: f(0))
        pl.when(g == 1)(lambda: f(1))

    def line(i, zz, back, core):
        if core == 0:
            return xbs[i].at[zz, :, wrap(y - back, NY), :, half(0)]
        return xbs[i].at[zz, wrap(x - back, NX), :, :, half(1)]

    def z_step(dz, core):
        if dz == 4:
            return 2 if core == 0 else -2
        return {1: 1, 2: 2, 3: 1, 5: -1, 6: -2, 7: -1}[dz]

    def z_send(i, dz, core):
        step = z_step(dz, core)
        ref = line(i, wrap(z - dz + (step if step > 0 else step + NZ), NZ), 0, core)
        return pltpu.make_async_remote_copy(
            src_ref=ref,
            dst_ref=ref,
            send_sem=z_sem.at[0, i, dz],
            recv_sem=z_sem.at[1, i, dz],
            device_id=device(wrap(z + step, NZ), x, y, core),
            device_id_type=MESH,
        )

    def z_arrival(i, dz, core):
        ref = line(i, wrap(z - dz, NZ), 0, core)
        return pltpu.make_async_remote_copy(
            src_ref=ref,
            dst_ref=ref,
            send_sem=z_sem.at[0, i, dz],
            recv_sem=z_sem.at[1, i, dz],
            device_id=device(wrap(z + z_step(dz, core), NZ), x, y, core),
            device_id_type=MESH,
        )

    def third_copy(i, dz, d, back, core):
        ref = line(i, wrap(z - dz, NZ), back, core)
        xx, yy = (x, wrap(y + d, NY)) if core == 0 else (wrap(x + d, NX), y)
        return pltpu.make_async_remote_copy(
            src_ref=ref,
            dst_ref=ref,
            send_sem=t_sem.at[0, i, dz, d],
            recv_sem=t_sem.at[1, i, dz, d],
            device_id=device(z, xx, yy, core),
            device_id_type=MESH,
        )

    def across(i, dz, core):
        ref = xbs[i].at[wrap(z - dz, NZ), :, :, :, half(core)]
        return pltpu.make_async_remote_copy(
            src_ref=ref,
            dst_ref=ref,
            send_sem=p_sem.at[0, i, dz],
            recv_sem=p_sem.at[1, i, dz],
            device_id=partner,
            device_id_type=MESH,
        )

    def send_z(i):
        def go(core):
            for dz in (1, 7, 2, 6):
                z_send(i, dz, core).start()

        by_core(go)

    def pass_line(i, s):
        def go(core):
            dz = ORDER[s]
            if s:
                z_arrival(i, dz, core).wait_recv()
            for later in ((3, 4) if core == 0 else (3,)) if dz == 2 else ():
                z_send(i, later, core).start()
            for later in ((5,) if core == 0 else (5, 4)) if dz == 6 else ():
                z_send(i, later, core).start()
            for d in (2, 1, 3):
                third_copy(i, dz, d, 0, core).start()

        by_core(go)

    def pass_plane(i, s):
        def go(core):
            dz = ORDER[s]
            for d in (1, 3, 2):
                third_copy(i, dz, d, d, core).wait_recv()

        by_core(go)
        across(i, ORDER[s], g).start()

    def wait_plane(i, s):
        across(i, ORDER[s], 1 - g).wait_recv()

    def finish_sends(i):
        def go(core):
            for dz in ORDER:
                if dz:
                    z_send(i, dz, core).wait_send()
                for d in range(1, NS):
                    third_copy(i, dz, d, 0, core).wait_send()

        by_core(go)
        for dz in ORDER:
            across(i, dz, g).wait_send()

    def prepare():
        for k in range(count // LANES):
            rows_k = slice(k * LANES, (k + 1) * LANES)
            table = tab[rows_k, :]
            cb16[rows_k, :] = table.astype(jnp.bfloat16)
            q = jnp.sum(table * table, axis=1, keepdims=True) * (SHARP * LOG2E)
            qb[rows_k, :] = jnp.broadcast_to(q, (LANES, LANES))

    def tile_dot(i, s, t=None):
        t = wrap(z - ORDER[s], NZ) if t is None else t
        tile = xbs[i][t].reshape(NX * NY * 16, D)
        sbs[s % 2][...] = lax.dot_general(
            cb16[...], tile, (((1,), (1,)), ((), ())), preferred_element_type=jnp.float32
        )

    def tile_soft(i, s, t=None):
        t = wrap(z - ORDER[s], NZ) if t is None else t
        for h in range(2):
            cut = slice(h * LANES, (h + 1) * LANES)
            score = sbs[s % 2][:, cut] * (2.0 * SHARP * LOG2E) - qb[...]
            top = jnp.max(score, axis=0, keepdims=True)
            e = jnp.exp2(score - top)
            total = jnp.sum(e, axis=0, keepdims=True)
            ebuf[2 * t + h] = e
            mbuf[pl.ds(2 * t + h, 1), :] = top
            lbuf[i, pl.ds(2 * t + h, 1), :] = top + jnp.log2(total)

    def merge(parts):
        top = parts[0]
        for part in parts[1:]:
            top = jnp.maximum(top, part)
        total = jnp.exp2(parts[0] - top)
        for part in parts[1:]:
            total = total + jnp.exp2(part - top)
        return top + jnp.log2(total)

    def role(h):
        return g if h == 0 else 1 - g

    def stat_one(i, d, h):
        r = role(h)
        return pltpu.make_async_remote_copy(
            src_ref=lbuf.at[i, pl.ds(8 * h, 8)],
            dst_ref=st1.at[i, d, r],
            send_sem=a_sem.at[0, i, d, r],
            recv_sem=a_sem.at[1, i, d, r],
            device_id=device(wrap(z + d, NZ), x, y, h),
            device_id_type=MESH,
        )

    def stat_arrival(i, d, r):
        return pltpu.make_async_remote_copy(
            src_ref=lbuf.at[i, pl.ds(0, 8)],
            dst_ref=st1.at[i, d, r],
            send_sem=a_sem.at[0, i, d, r],
            recv_sem=a_sem.at[1, i, d, r],
            device_id=partner,
            device_id_type=MESH,
        )

    def stat_two(i, dx, dy, r):
        gg = g if r == 0 else 1 - g
        return pltpu.make_async_remote_copy(
            src_ref=merged.at[i],
            dst_ref=st2.at[i, dx, dy, r],
            send_sem=b_sem.at[0, i, dx, dy, r],
            recv_sem=b_sem.at[1, i, dx, dy, r],
            device_id=device(z, wrap(x + dx, NX), wrap(y + dy, NY), gg),
            device_id_type=MESH,
        )

    def stat_result(i, dx, dy, h):
        r = role(h)
        return pltpu.make_async_remote_copy(
            src_ref=merged.at[i],
            dst_ref=st2.at[i, dx, dy, r],
            send_sem=b_sem.at[0, i, dx, dy, r],
            recv_sem=b_sem.at[1, i, dx, dy, r],
            device_id=partner,
            device_id_type=MESH,
        )

    far = sorted(
        [(dx, dy) for dx in range(NX) for dy in range(NY)],
        key=lambda v: -(min(v[0], NX - v[0]) + min(v[1], NY - v[1])),
    )
    ones = [(d, r) for d in (4, 3, 5, 2, 6, 1, 7, 0) for r in range(2) if d or r]
    twos = [(dx, dy, r) for dx, dy in far for r in range(2) if dx or dy or r]

    def send_stats(i, h):
        for d in (4, 3, 5, 2, 6, 1, 7):
            stat_one(i, d, h).start()

        @pl.when(g == h)
        def _():
            st1[i, 0, 0] = lbuf[i, 8 * h : 8 * h + 8, :]

        @pl.when(g != h)
        def _():
            stat_one(i, 0, h).start()

    def spread_stats(i):
        for d, r in ones:
            stat_arrival(i, d, r).wait_recv()
        total = merge([st1[i, d, r] for d in range(NZ) for r in range(2)])
        merged[i] = total
        for dx, dy, r in twos:
            stat_two(i, dx, dy, r).start()
        st2[i, 0, 0, 0] = total

    def take_stats(i, h):
        for dx, dy in far[:-1]:
            stat_result(i, dx, dy, h).wait_recv()

        @pl.when(g != h)
        def _():
            stat_result(i, 0, 0, h).wait_recv()

        r = role(h)
        final = merge([st2[i, dx, dy, r] for dx, dy in far])
        fin[i, 8 * h : 8 * h + 8, :] = final
        return final

    def finish_stats(i):
        for d, r in ones:
            stat_arrival(i, d, r).wait_send()
        for dx, dy, r in twos:
            stat_two(i, dx, dy, r).wait_send()

    def reseeding(i):
        def look(j, carry):
            place, row = carry
            here = ids[i, j] - cent * (2 * count)
            inside = (here >= 0) & (here < 2 * count)
            pick = ids[2 * ITERS + i, j] * 1024 + ids[ITERS + i, j]
            return place + jnp.where(inside, here, 0), row + jnp.where(inside, pick, 0)

        place, row = lax.fori_loop(0, ids.shape[1], look, (jnp.int32(0), jnp.int32(0)))
        group = lax.div(row, 1024)
        inner = lax.rem(row, 1024)
        return place - base, group, inner

    def picked_row(i, group, inner):
        c = lax.div(inner, 8)
        block = xbs[i][lax.div(c, NX * NY), lax.rem(lax.div(c, NY), NX), lax.rem(c, NY)]
        which = lax.broadcasted_iota(jnp.int32, (16, D), 0) == group * 8 + lax.rem(inner, 8)
        return jnp.sum(jnp.where(which, block.astype(jnp.float32), 0.0), axis=0, keepdims=True)

    def update(i, h, final, picked, place, done):
        fac = jnp.exp2(mbuf[8 * h : 8 * h + 8, :] - final)
        rows = NZ * NX * NY * 8
        xhalf = xbs[i].at[pl.ds(h * (NZ // 2), NZ // 2)].reshape(rows, D)
        for k, (at, size) in enumerate(PARTS):
            rows_k = slice(at, at + size)
            part = jnp.zeros((size, LANES), jnp.float32)
            for t in range(NZ):
                w = (ebuf[8 * h + t, rows_k, :] * fac[t : t + 1, :]).astype(jnp.bfloat16)
                wbuf[rows_k, h * rows + t * LANES : h * rows + (t + 1) * LANES] = w
                part = part + w.astype(jnp.float32)
            total = jnp.dot(
                wbuf[rows_k, h * rows : (h + 1) * rows], xhalf[...], preferred_element_type=jnp.float32
            )
            if h == 0:
                tally[rows_k, :] = part
                sums[rows_k, :] = total
                continue
            counts = jnp.sum(tally[rows_k, :] + part, axis=1, keepdims=True)
            table = tab[rows_k, :]
            table = table + (sums[rows_k, :] + total - counts * table) * (1.0 / (counts + 0.05))
            spot = lax.broadcasted_iota(jnp.int32, (size, D), 0) + at
            tab[rows_k, :] = jnp.where(spot == place, picked, table)
            done(k)

    def write_energy(i):
        offset = (x * NY + y) * 16 + g * 8
        row = fin[i, pl.ds(2 * z + lax.div(offset, LANES), 1), :]
        row = pltpu.roll(row, wrap(-lax.rem(offset, LANES), LANES), 1)
        energy[i] = row[:, :8] * (1.0 / (LOG2E * SHARP * D))

    def results(k):
        at, size = PARTS[k]
        part = out.at[pl.ds(pl.multiple_of(base + at, LANES), size)]
        mine = tab.at[pl.ds(at, size)]
        keep = pltpu.make_async_copy(mine, part, o_sem.at[0, k])
        give = pltpu.make_async_remote_copy(
            src_ref=mine,
            dst_ref=part,
            send_sem=o_sem.at[1, k],
            recv_sem=o_sem.at[2, k],
            device_id=partner,
            device_id_type=MESH,
        )
        return keep, give

    def send_result(k):
        for copy in results(k):
            copy.start()

    place_line()
    send_z(0)
    pass_line(0, 0)
    loads[2].wait()
    prepare()
    for s in range(1, NZ + LAG3 + LAGP + 1):
        if s < NZ:
            pass_line(0, s)
        if 0 <= s - LAG3 < NZ:
            pass_plane(0, s - LAG3)
        if s == 5:
            send_z(1)
        if 10 <= s < 13:
            pass_line(1, s - 10)
        done = s - LAG3 - LAGP
        if 0 <= done < NZ:
            wait_plane(0, done)
            tile_dot(0, done)
        if 0 <= done - 1:
            tile_soft(0, done - 1)

    send_stats(0, 0)
    send_stats(0, 1)
    pass_line(1, 3)
    pass_line(1, 4)
    loads[1].wait()
    places = [reseeding(i) for i in range(ITERS)]
    for s in range(3):
        pass_plane(1, s)
    for s in range(5, NZ):
        pass_line(1, s)
    spread_stats(0)
    for s in range(3, 6):
        pass_plane(1, s)
    place, group, inner = places[0]
    picked = picked_row(0, group, inner)
    for h in range(2):
        update(0, h, take_stats(0, h), picked, place, lambda k: None)
    for s in range(6, NZ):
        pass_plane(1, s)
    prepare()

    for s in range(NZ):
        wait_plane(1, s)
    for t in range(NZ + 1):
        if t < NZ:
            tile_dot(1, t, t)
        if t:
            tile_soft(1, t - 1, t - 1)
        if t == NZ // 2:
            send_stats(1, 0)
    send_stats(1, 1)
    place, group, inner = places[1]
    picked = picked_row(1, group, inner)
    spread_stats(1)
    for h in range(2):
        update(1, h, take_stats(1, h), picked, place, send_result)

    write_energy(0)
    write_energy(1)
    for d, h in firsts:
        first_copy(d, h).wait_send()
    for i in range(ITERS):
        finish_sends(i)
        finish_stats(i)
    for k in range(len(PARTS)):
        keep, give = results(k)
        keep.wait()
        give.wait()


def shards(codebook, batch, dead_ids, reseed_rows, source_group):
    ids = jnp.concatenate([dead_ids, reseed_rows, source_group], axis=0)
    held = codebook.shape[0]
    count = held // 2
    anywhere = pl.BlockSpec(memory_space=pl.ANY)
    rows = NZ * NX * NY * 16
    dma = pltpu.SemaphoreType.DMA
    vmem = pltpu.VMEM
    table, energies = pl.pallas_call(
        kernel,
        out_shape=(
            jax.ShapeDtypeStruct((held, D), jnp.float32),
            jax.ShapeDtypeStruct((ITERS, 1, 8), jnp.float32),
        ),
        in_specs=[pl.BlockSpec(memory_space=pltpu.HBM)] * 3,
        out_specs=(anywhere, pl.BlockSpec(memory_space=vmem)),
        scratch_shapes=[
            vmem((NZ, NX, NY, 16, D), jnp.bfloat16),
            vmem((NZ, NX, NY, 16, D), jnp.bfloat16),
            vmem(batch.shape, batch.dtype),
            pltpu.SMEM(ids.shape, ids.dtype),
            vmem((16, D), jnp.bfloat16),
            vmem((NS, 2, 16, HALF), jnp.bfloat16),
            vmem((count, D), jnp.float32),
            vmem((count, D), jnp.bfloat16),
            vmem((count, LANES), jnp.float32),
            vmem((count, 2 * LANES), jnp.float32),
            vmem((count, 2 * LANES), jnp.float32),
            vmem((2 * NZ, count, LANES), jnp.float32),
            vmem((count, rows), jnp.bfloat16),
            vmem((count, D), jnp.float32),
            vmem((count, LANES), jnp.float32),
            vmem((2 * NZ, LANES), jnp.float32),
            vmem((ITERS, 2 * NZ, LANES), jnp.float32),
            vmem((ITERS, 2 * NZ, LANES), jnp.float32),
            vmem((ITERS, 8, LANES), jnp.float32),
            vmem((ITERS, NZ, 2, 8, LANES), jnp.float32),
            vmem((ITERS, NX, NY, 2, 8, LANES), jnp.float32),
            dma((3,)),
            dma((2, NS, 2)),
            dma((2, ITERS, NZ)),
            dma((2, ITERS, NZ, NS)),
            dma((2, ITERS, NZ)),
            dma((2, ITERS, NZ, 2)),
            dma((2, ITERS, NX, NY, 2)),
            dma((3, len(PARTS))),
        ],
        compiler_params=pltpu.CompilerParams(
            collective_id=0, has_side_effects=True, vmem_limit_bytes=48 * 2**20
        ),
        name="soft_kmeans",
    )(codebook, batch, ids)
    return (table, energies)


def solution(mesh):
    return jax.shard_map(
        shards,
        mesh=mesh,
        in_specs=(P("cent", None), P(None, "rows", "cent", None), P(), P(), P()),
        out_specs=(P("cent", None), P(None, "rows", "cent")),
        check_vma=False,
    )
```

```python
import math

import jax
import jax.numpy as jnp
from jax import lax
from jax.experimental import pallas as pl
from jax.experimental.pallas import tpu as pltpu
from jax.sharding import PartitionSpec as P

D = 768
ITERS = 2
NZ, NX, NY = 8, 4, 4
NS = 4
HALF = D // 2
SHARP = 5.0 / math.sqrt(D)
LOG2E = 1.0 / math.log(2.0)
MESH = pl.DeviceIdType.MESH
LANES = 128
PARTS = ((0, 256), (256, 256))
ORDER = (0, 1, 7, 2, 6, 3, 5, 4)
LAG3, LAGP = 4, 2


def wrap(value, size):
    return lax.rem(value + size, size)


def kernel(
    book,
    batch_in,
    ids_in,
    out,
    energy,
    xb0,
    xb1,
    batch,
    ids,
    own16,
    first,
    tab,
    cb16,
    qb,
    sb0,
    sb1,
    ebuf,
    wbuf,
    sums,
    tally,
    mbuf,
    lbuf,
    fin,
    merged,
    st1,
    st2,
    load_sem,
    f_sem,
    z_sem,
    t_sem,
    p_sem,
    a_sem,
    b_sem,
    o_sem,
):
    cent = lax.axis_index("cent")
    g = lax.axis_index("rows")
    z = lax.div(cent, NX * NY)
    x = lax.rem(lax.div(cent, NY), NX)
    y = lax.rem(cent, NY)
    xbs = (xb0, xb1)
    sbs = (sb0, sb1)
    count = tab.shape[0]
    base = g * count

    def half(core):
        return pl.ds(pl.multiple_of(core * HALF, LANES), HALF)

    def device(zz, xx, yy, gg):
        return (zz * (NX * NY) + xx * NY + yy, gg)

    def along(core, d):
        return wrap(x + (1 - core) * d, NX), wrap(y + core * d, NY)

    partner = device(z, x, y, 1 - g)

    loads = [
        pltpu.make_async_copy(batch_in, batch, load_sem.at[0]),
        pltpu.make_async_copy(ids_in, ids, load_sem.at[1]),
        pltpu.make_async_copy(
            book.at[pl.ds(pl.multiple_of(base, 256), count)], tab, load_sem.at[2]
        ),
    ]
    for load in loads:
        load.start()

    barrier = pltpu.get_barrier_semaphore()

    def greet(to):
        pl.semaphore_signal(barrier, inc=1, device_id=to, device_id_type=MESH)

    for d in (1, 2, NZ - 2, NZ - 1):
        greet(device(wrap(z + d, NZ), x, y, g))
    for d in range(1, NS):
        for gg in (g, 1 - g):
            greet(device(z, wrap(x + d, NX), y, gg))
            greet(device(z, x, wrap(y + d, NY), gg))
    greet(partner)
    loads[0].wait()
    own16[...] = jnp.concatenate(
        [batch[0, 0].astype(jnp.float32), batch[1, 0].astype(jnp.float32)], axis=0
    ).astype(jnp.bfloat16)
    pl.semaphore_wait(barrier, 4 + 4 * (NS - 1) + 1)

    def first_copy(d, h):
        core = g if h == 0 else 1 - g
        xx, yy = along(core, d)
        return pltpu.make_async_remote_copy(
            src_ref=own16.at[:, half(core)],
            dst_ref=first.at[d, h],
            send_sem=f_sem.at[0, d, h],
            recv_sem=f_sem.at[1, d, h],
            device_id=device(z, xx, yy, core),
            device_id_type=MESH,
        )

    firsts = [(d, h) for d in (2, 1, 3, 0) for h in range(2) if d or h]
    for d, h in firsts:
        first_copy(d, h).start()
    first[0, 0] = own16[:, half(g)]

    def place_line():
        for d, h in firsts:
            first_copy(d, h).wait_recv()
        for d in range(NS):
            same = first[d, 0].astype(jnp.float32)
            other = first[d, 1].astype(jnp.float32)
            xx, yy = along(g, -d)
            for i in range(ITERS):
                rows_i = slice(8 * i, 8 * i + 8)
                a = jnp.where(g == 0, same[rows_i], other[rows_i])
                b = jnp.where(g == 0, other[rows_i], same[rows_i])
                block = jnp.concatenate([a, b], axis=0).astype(jnp.bfloat16)
                xbs[i][z, xx, yy, :, half(g)] = block

    def by_core(f):
        pl.when(g == 0)(lambda: f(0))
        pl.when(g == 1)(lambda: f(1))

    def line(i, zz, back, core):
        if core == 0:
            return xbs[i].at[zz, :, wrap(y - back, NY), :, half(0)]
        return xbs[i].at[zz, wrap(x - back, NX), :, :, half(1)]

    def z_step(dz, core):
        if dz == 4:
            return 2 if core == 0 else -2
        return {1: 1, 2: 2, 3: 1, 5: -1, 6: -2, 7: -1}[dz]

    def z_send(i, dz, core):
        step = z_step(dz, core)
        ref = line(i, wrap(z - dz + (step if step > 0 else step + NZ), NZ), 0, core)
        return pltpu.make_async_remote_copy(
            src_ref=ref,
            dst_ref=ref,
            send_sem=z_sem.at[0, i, dz],
            recv_sem=z_sem.at[1, i, dz],
            device_id=device(wrap(z + step, NZ), x, y, core),
            device_id_type=MESH,
        )

    def z_arrival(i, dz, core):
        ref = line(i, wrap(z - dz, NZ), 0, core)
        return pltpu.make_async_remote_copy(
            src_ref=ref,
            dst_ref=ref,
            send_sem=z_sem.at[0, i, dz],
            recv_sem=z_sem.at[1, i, dz],
            device_id=device(wrap(z + z_step(dz, core), NZ), x, y, core),
            device_id_type=MESH,
        )

    def third_copy(i, dz, d, back, core):
        ref = line(i, wrap(z - dz, NZ), back, core)
        xx, yy = (x, wrap(y + d, NY)) if core == 0 else (wrap(x + d, NX), y)
        return pltpu.make_async_remote_copy(
            src_ref=ref,
            dst_ref=ref,
            send_sem=t_sem.at[0, i, dz, d],
            recv_sem=t_sem.at[1, i, dz, d],
            device_id=device(z, xx, yy, core),
            device_id_type=MESH,
        )

    def across(i, dz, core):
        ref = xbs[i].at[wrap(z - dz, NZ), :, :, :, half(core)]
        return pltpu.make_async_remote_copy(
            src_ref=ref,
            dst_ref=ref,
            send_sem=p_sem.at[0, i, dz],
            recv_sem=p_sem.at[1, i, dz],
            device_id=partner,
            device_id_type=MESH,
        )

    def send_z(i):
        def go(core):
            for dz in (1, 7, 2, 6):
                z_send(i, dz, core).start()

        by_core(go)

    def pass_line(i, s):
        def go(core):
            dz = ORDER[s]
            if s:
                z_arrival(i, dz, core).wait_recv()
            for later in ((3, 4) if core == 0 else (3,)) if dz == 2 else ():
                z_send(i, later, core).start()
            for later in ((5,) if core == 0 else (5, 4)) if dz == 6 else ():
                z_send(i, later, core).start()
            for d in (2, 1, 3):
                third_copy(i, dz, d, 0, core).start()

        by_core(go)

    def pass_plane(i, s):
        def go(core):
            dz = ORDER[s]
            for d in (1, 3, 2):
                third_copy(i, dz, d, d, core).wait_recv()

        by_core(go)
        across(i, ORDER[s], g).start()

    def wait_plane(i, s):
        across(i, ORDER[s], 1 - g).wait_recv()

    def finish_sends(i):
        def go(core):
            for dz in ORDER:
                if dz:
                    z_send(i, dz, core).wait_send()
                for d in range(1, NS):
                    third_copy(i, dz, d, 0, core).wait_send()

        by_core(go)
        for dz in ORDER:
            across(i, dz, g).wait_send()

    def prepare():
        for k in range(count // LANES):
            rows_k = slice(k * LANES, (k + 1) * LANES)
            table = tab[rows_k, :]
            cb16[rows_k, :] = table.astype(jnp.bfloat16)
            q = jnp.sum(table * table, axis=1, keepdims=True) * (SHARP * LOG2E)
            qb[rows_k, :] = jnp.broadcast_to(q, (LANES, LANES))

    def tile_dot(i, s, t=None):
        t = wrap(z - ORDER[s], NZ) if t is None else t
        tile = xbs[i][t].reshape(NX * NY * 16, D)
        sbs[s % 2][...] = lax.dot_general(
            cb16[...], tile, (((1,), (1,)), ((), ())), preferred_element_type=jnp.float32
        )

    def tile_soft(i, s, t=None):
        t = wrap(z - ORDER[s], NZ) if t is None else t
        for h in range(2):
            cut = slice(h * LANES, (h + 1) * LANES)
            score = sbs[s % 2][:, cut] * (2.0 * SHARP * LOG2E) - qb[...]
            top = jnp.max(score, axis=0, keepdims=True)
            e = jnp.exp2(score - top)
            total = jnp.sum(e, axis=0, keepdims=True)
            ebuf[2 * t + h] = e
            mbuf[pl.ds(2 * t + h, 1), :] = top
            lbuf[i, pl.ds(2 * t + h, 1), :] = top + jnp.log2(total)

    def merge(parts):
        top = parts[0]
        for part in parts[1:]:
            top = jnp.maximum(top, part)
        total = jnp.exp2(parts[0] - top)
        for part in parts[1:]:
            total = total + jnp.exp2(part - top)
        return top + jnp.log2(total)

    def role(h):
        return g if h == 0 else 1 - g

    def stat_one(i, d, h):
        r = role(h)
        return pltpu.make_async_remote_copy(
            src_ref=lbuf.at[i, pl.ds(8 * h, 8)],
            dst_ref=st1.at[i, d, r],
            send_sem=a_sem.at[0, i, d, r],
            recv_sem=a_sem.at[1, i, d, r],
            device_id=device(wrap(z + d, NZ), x, y, h),
            device_id_type=MESH,
        )

    def stat_arrival(i, d, r):
        return pltpu.make_async_remote_copy(
            src_ref=lbuf.at[i, pl.ds(0, 8)],
            dst_ref=st1.at[i, d, r],
            send_sem=a_sem.at[0, i, d, r],
            recv_sem=a_sem.at[1, i, d, r],
            device_id=partner,
            device_id_type=MESH,
        )

    def stat_two(i, dx, dy, r):
        gg = g if r == 0 else 1 - g
        return pltpu.make_async_remote_copy(
            src_ref=merged.at[i],
            dst_ref=st2.at[i, dx, dy, r],
            send_sem=b_sem.at[0, i, dx, dy, r],
            recv_sem=b_sem.at[1, i, dx, dy, r],
            device_id=device(z, wrap(x + dx, NX), wrap(y + dy, NY), gg),
            device_id_type=MESH,
        )

    def stat_result(i, dx, dy, h):
        r = role(h)
        return pltpu.make_async_remote_copy(
            src_ref=merged.at[i],
            dst_ref=st2.at[i, dx, dy, r],
            send_sem=b_sem.at[0, i, dx, dy, r],
            recv_sem=b_sem.at[1, i, dx, dy, r],
            device_id=partner,
            device_id_type=MESH,
        )

    far = sorted(
        [(dx, dy) for dx in range(NX) for dy in range(NY)],
        key=lambda v: -(min(v[0], NX - v[0]) + min(v[1], NY - v[1])),
    )
    ones = [(d, r) for d in (4, 3, 5, 2, 6, 1, 7, 0) for r in range(2) if d or r]
    twos = [(dx, dy, r) for dx, dy in far for r in range(2) if dx or dy or r]

    def send_stats(i, h):
        for d in (4, 3, 5, 2, 6, 1, 7):
            stat_one(i, d, h).start()

        @pl.when(g == h)
        def _():
            st1[i, 0, 0] = lbuf[i, 8 * h : 8 * h + 8, :]

        @pl.when(g != h)
        def _():
            stat_one(i, 0, h).start()

    def spread_stats(i):
        for d, r in ones:
            stat_arrival(i, d, r).wait_recv()
        total = merge([st1[i, d, r] for d in range(NZ) for r in range(2)])
        merged[i] = total
        for dx, dy, r in twos:
            stat_two(i, dx, dy, r).start()
        st2[i, 0, 0, 0] = total

    def take_stats(i, h):
        for dx, dy in far[:-1]:
            stat_result(i, dx, dy, h).wait_recv()

        @pl.when(g != h)
        def _():
            stat_result(i, 0, 0, h).wait_recv()

        r = role(h)
        final = merge([st2[i, dx, dy, r] for dx, dy in far])
        fin[i, 8 * h : 8 * h + 8, :] = final
        return final

    def finish_stats(i):
        for d, r in ones:
            stat_arrival(i, d, r).wait_send()
        for dx, dy, r in twos:
            stat_two(i, dx, dy, r).wait_send()

    def reseeding(i):
        def look(j, carry):
            place, row = carry
            here = ids[i, j] - cent * (2 * count)
            inside = (here >= 0) & (here < 2 * count)
            pick = ids[2 * ITERS + i, j] * 1024 + ids[ITERS + i, j]
            return place + jnp.where(inside, here, 0), row + jnp.where(inside, pick, 0)

        place, row = lax.fori_loop(0, ids.shape[1], look, (jnp.int32(0), jnp.int32(0)))
        group = lax.div(row, 1024)
        inner = lax.rem(row, 1024)
        return place - base, group, inner

    def picked_row(i, group, inner):
        c = lax.div(inner, 8)
        block = xbs[i][lax.div(c, NX * NY), lax.rem(lax.div(c, NY), NX), lax.rem(c, NY)]
        which = lax.broadcasted_iota(jnp.int32, (16, D), 0) == group * 8 + lax.rem(inner, 8)
        return jnp.sum(jnp.where(which, block.astype(jnp.float32), 0.0), axis=0, keepdims=True)

    def update(i, h, final, picked, place, done):
        fac = jnp.exp2(mbuf[8 * h : 8 * h + 8, :] - final)
        rows = NZ * NX * NY * 8
        xhalf = xbs[i].at[pl.ds(h * (NZ // 2), NZ // 2)].reshape(rows, D)
        for k, (at, size) in enumerate(PARTS):
            rows_k = slice(at, at + size)
            part = jnp.zeros((size, LANES), jnp.float32)
            for t in range(NZ):
                w = (ebuf[8 * h + t, rows_k, :] * fac[t : t + 1, :]).astype(jnp.bfloat16)
                wbuf[rows_k, h * rows + t * LANES : h * rows + (t + 1) * LANES] = w
                part = part + w.astype(jnp.float32)
            total = jnp.dot(
                wbuf[rows_k, h * rows : (h + 1) * rows], xhalf[...], preferred_element_type=jnp.float32
            )
            if h == 0:
                tally[rows_k, :] = part
                sums[rows_k, :] = total
                continue
            counts = jnp.sum(tally[rows_k, :] + part, axis=1, keepdims=True)
            table = tab[rows_k, :]
            table = table + (sums[rows_k, :] + total - counts * table) * (1.0 / (counts + 0.05))
            spot = lax.broadcasted_iota(jnp.int32, (size, D), 0) + at
            tab[rows_k, :] = jnp.where(spot == place, picked, table)
            done(k)

    def write_energy(i):
        offset = (x * NY + y) * 16 + g * 8
        row = fin[i, pl.ds(2 * z + lax.div(offset, LANES), 1), :]
        row = pltpu.roll(row, wrap(-lax.rem(offset, LANES), LANES), 1)
        energy[i] = row[:, :8] * (1.0 / (LOG2E * SHARP * D))

    def results(k):
        at, size = PARTS[k]
        part = out.at[pl.ds(pl.multiple_of(base + at, LANES), size)]
        mine = tab.at[pl.ds(at, size)]
        keep = pltpu.make_async_copy(mine, part, o_sem.at[0, k])
        give = pltpu.make_async_remote_copy(
            src_ref=mine,
            dst_ref=part,
            send_sem=o_sem.at[1, k],
            recv_sem=o_sem.at[2, k],
            device_id=partner,
            device_id_type=MESH,
        )
        return keep, give

    def send_result(k):
        for copy in results(k):
            copy.start()

    place_line()
    send_z(0)
    pass_line(0, 0)
    pass_line(1, 0)
    loads[2].wait()
    prepare()
    for s in range(1, NZ + LAG3 + LAGP + 1):
        if s < NZ:
            pass_line(0, s)
        if 0 <= s - LAG3 < NZ:
            pass_plane(0, s - LAG3)
        if s == 5:
            send_z(1)
        if 8 <= s < 12:
            pass_line(1, s - 7)
        done = s - LAG3 - LAGP
        if 0 <= done < NZ:
            wait_plane(0, done)
            tile_dot(0, done)
        if 0 <= done - 1:
            tile_soft(0, done - 1)

    send_stats(0, 0)
    send_stats(0, 1)
    loads[1].wait()
    places = [reseeding(i) for i in range(ITERS)]
    for s in range(5, NZ):
        pass_line(1, s)
    for s in range(5):
        pass_plane(1, s)
    spread_stats(0)
    for s in range(5, NZ):
        pass_plane(1, s)
    place, group, inner = places[0]
    picked = picked_row(0, group, inner)
    for h in range(2):
        update(0, h, take_stats(0, h), picked, place, lambda k: None)
    prepare()

    for s in range(NZ):
        wait_plane(1, s)
    for t in range(NZ + 1):
        if t < NZ:
            tile_dot(1, t, t)
        if t:
            tile_soft(1, t - 1, t - 1)
        if t == NZ // 2:
            send_stats(1, 0)
    send_stats(1, 1)
    place, group, inner = places[1]
    picked = picked_row(1, group, inner)
    spread_stats(1)
    for h in range(2):
        update(1, h, take_stats(1, h), picked, place, send_result)

    write_energy(0)
    write_energy(1)
    for d, h in firsts:
        first_copy(d, h).wait_send()
    for i in range(ITERS):
        finish_sends(i)
        finish_stats(i)
    for k in range(len(PARTS)):
        keep, give = results(k)
        keep.wait()
        give.wait()


def shards(codebook, batch, dead_ids, reseed_rows, source_group):
    ids = jnp.concatenate([dead_ids, reseed_rows, source_group], axis=0)
    held = codebook.shape[0]
    count = held // 2
    anywhere = pl.BlockSpec(memory_space=pl.ANY)
    rows = NZ * NX * NY * 16
    dma = pltpu.SemaphoreType.DMA
    vmem = pltpu.VMEM
    table, energies = pl.pallas_call(
        kernel,
        out_shape=(
            jax.ShapeDtypeStruct((held, D), jnp.float32),
            jax.ShapeDtypeStruct((ITERS, 1, 8), jnp.float32),
        ),
        in_specs=[pl.BlockSpec(memory_space=pltpu.HBM)] * 3,
        out_specs=(anywhere, pl.BlockSpec(memory_space=vmem)),
        scratch_shapes=[
            vmem((NZ, NX, NY, 16, D), jnp.bfloat16),
            vmem((NZ, NX, NY, 16, D), jnp.bfloat16),
            vmem(batch.shape, batch.dtype),
            pltpu.SMEM(ids.shape, ids.dtype),
            vmem((16, D), jnp.bfloat16),
            vmem((NS, 2, 16, HALF), jnp.bfloat16),
            vmem((count, D), jnp.float32),
            vmem((count, D), jnp.bfloat16),
            vmem((count, LANES), jnp.float32),
            vmem((count, 2 * LANES), jnp.float32),
            vmem((count, 2 * LANES), jnp.float32),
            vmem((2 * NZ, count, LANES), jnp.float32),
            vmem((count, rows), jnp.bfloat16),
            vmem((count, D), jnp.float32),
            vmem((count, LANES), jnp.float32),
            vmem((2 * NZ, LANES), jnp.float32),
            vmem((ITERS, 2 * NZ, LANES), jnp.float32),
            vmem((ITERS, 2 * NZ, LANES), jnp.float32),
            vmem((ITERS, 8, LANES), jnp.float32),
            vmem((ITERS, NZ, 2, 8, LANES), jnp.float32),
            vmem((ITERS, NX, NY, 2, 8, LANES), jnp.float32),
            dma((3,)),
            dma((2, NS, 2)),
            dma((2, ITERS, NZ)),
            dma((2, ITERS, NZ, NS)),
            dma((2, ITERS, NZ)),
            dma((2, ITERS, NZ, 2)),
            dma((2, ITERS, NX, NY, 2)),
            dma((3, len(PARTS))),
        ],
        compiler_params=pltpu.CompilerParams(
            collective_id=0, has_side_effects=True, vmem_limit_bytes=48 * 2**20
        ),
        name="soft_kmeans",
    )(codebook, batch, ids)
    return (table, energies)


def solution(mesh):
    return jax.shard_map(
        shards,
        mesh=mesh,
        in_specs=(P("cent", None), P(None, "rows", "cent", None), P(), P(), P()),
        out_specs=(P("cent", None), P(None, "rows", "cent")),
        check_vma=False,
    )
```

```python
import math

import jax
import jax.numpy as jnp
from jax import lax
from jax.experimental import pallas as pl
from jax.experimental.pallas import tpu as pltpu
from jax.sharding import PartitionSpec as P

D = 768
ITERS = 2
NZ, NX, NY = 8, 4, 4
NS = 4
HALF = D // 2
SHARP = 5.0 / math.sqrt(D)
LOG2E = 1.0 / math.log(2.0)
MESH = pl.DeviceIdType.MESH
LANES = 128
PARTS = ((0, 256), (256, 256))
ORDER = (0, 1, 7, 2, 6, 3, 5, 4)
LAG3, LAGP = 4, 2


def wrap(value, size):
    return lax.rem(value + size, size)


def kernel(
    book,
    batch_in,
    ids_in,
    out,
    energy,
    xb0,
    xb1,
    batch,
    ids,
    own16,
    first,
    tab,
    cb16,
    qb,
    sb0,
    sb1,
    ebuf,
    wbuf,
    sums,
    tally,
    mbuf,
    lbuf,
    fin,
    merged,
    st1,
    st2,
    load_sem,
    f_sem,
    z_sem,
    t_sem,
    p_sem,
    a_sem,
    b_sem,
    o_sem,
):
    cent = lax.axis_index("cent")
    g = lax.axis_index("rows")
    z = lax.div(cent, NX * NY)
    x = lax.rem(lax.div(cent, NY), NX)
    y = lax.rem(cent, NY)
    xbs = (xb0, xb1)
    sbs = (sb0, sb1)
    count = tab.shape[0]
    base = g * count

    def half(core):
        return pl.ds(pl.multiple_of(core * HALF, LANES), HALF)

    def device(zz, xx, yy, gg):
        return (zz * (NX * NY) + xx * NY + yy, gg)

    def along(core, d):
        return wrap(x + (1 - core) * d, NX), wrap(y + core * d, NY)

    partner = device(z, x, y, 1 - g)

    loads = [
        pltpu.make_async_copy(batch_in, batch, load_sem.at[0]),
        pltpu.make_async_copy(ids_in, ids, load_sem.at[1]),
        pltpu.make_async_copy(
            book.at[pl.ds(pl.multiple_of(base, 256), count)], tab, load_sem.at[2]
        ),
    ]
    for load in loads:
        load.start()

    barrier = pltpu.get_barrier_semaphore()

    def greet(to):
        pl.semaphore_signal(barrier, inc=1, device_id=to, device_id_type=MESH)

    for d in (1, 2, NZ - 2, NZ - 1):
        greet(device(wrap(z + d, NZ), x, y, g))
    for d in range(1, NS):
        for gg in (g, 1 - g):
            greet(device(z, wrap(x + d, NX), y, gg))
            greet(device(z, x, wrap(y + d, NY), gg))
    greet(partner)
    loads[0].wait()
    own16[...] = jnp.concatenate(
        [batch[0, 0].astype(jnp.float32), batch[1, 0].astype(jnp.float32)], axis=0
    ).astype(jnp.bfloat16)
    pl.semaphore_wait(barrier, 4 + 4 * (NS - 1) + 1)

    def first_copy(d, h):
        core = g if h == 0 else 1 - g
        xx, yy = along(core, d)
        return pltpu.make_async_remote_copy(
            src_ref=own16.at[:, half(core)],
            dst_ref=first.at[d, h],
            send_sem=f_sem.at[0, d, h],
            recv_sem=f_sem.at[1, d, h],
            device_id=device(z, xx, yy, core),
            device_id_type=MESH,
        )

    firsts = [(d, h) for d in (2, 1, 3, 0) for h in range(2) if d or h]
    for d, h in firsts:
        first_copy(d, h).start()
    first[0, 0] = own16[:, half(g)]

    def place_line():
        for d, h in firsts:
            first_copy(d, h).wait_recv()
        for d in range(NS):
            same = first[d, 0].astype(jnp.float32)
            other = first[d, 1].astype(jnp.float32)
            xx, yy = along(g, -d)
            for i in range(ITERS):
                rows_i = slice(8 * i, 8 * i + 8)
                a = jnp.where(g == 0, same[rows_i], other[rows_i])
                b = jnp.where(g == 0, other[rows_i], same[rows_i])
                block = jnp.concatenate([a, b], axis=0).astype(jnp.bfloat16)
                xbs[i][z, xx, yy, :, half(g)] = block

    def by_core(f):
        pl.when(g == 0)(lambda: f(0))
        pl.when(g == 1)(lambda: f(1))

    def line(i, zz, back, core):
        if core == 0:
            return xbs[i].at[zz, :, wrap(y - back, NY), :, half(0)]
        return xbs[i].at[zz, wrap(x - back, NX), :, :, half(1)]

    def z_step(dz, core):
        if dz == 4:
            return 2 if core == 0 else -2
        return {1: 1, 2: 2, 3: 1, 5: -1, 6: -2, 7: -1}[dz]

    def z_send(i, dz, core):
        step = z_step(dz, core)
        ref = line(i, wrap(z - dz + (step if step > 0 else step + NZ), NZ), 0, core)
        return pltpu.make_async_remote_copy(
            src_ref=ref,
            dst_ref=ref,
            send_sem=z_sem.at[0, i, dz],
            recv_sem=z_sem.at[1, i, dz],
            device_id=device(wrap(z + step, NZ), x, y, core),
            device_id_type=MESH,
        )

    def z_arrival(i, dz, core):
        ref = line(i, wrap(z - dz, NZ), 0, core)
        return pltpu.make_async_remote_copy(
            src_ref=ref,
            dst_ref=ref,
            send_sem=z_sem.at[0, i, dz],
            recv_sem=z_sem.at[1, i, dz],
            device_id=device(wrap(z + z_step(dz, core), NZ), x, y, core),
            device_id_type=MESH,
        )

    def third_copy(i, dz, d, back, core):
        ref = line(i, wrap(z - dz, NZ), back, core)
        xx, yy = (x, wrap(y + d, NY)) if core == 0 else (wrap(x + d, NX), y)
        return pltpu.make_async_remote_copy(
            src_ref=ref,
            dst_ref=ref,
            send_sem=t_sem.at[0, i, dz, d],
            recv_sem=t_sem.at[1, i, dz, d],
            device_id=device(z, xx, yy, core),
            device_id_type=MESH,
        )

    def across(i, dz, core):
        ref = xbs[i].at[wrap(z - dz, NZ), :, :, :, half(core)]
        return pltpu.make_async_remote_copy(
            src_ref=ref,
            dst_ref=ref,
            send_sem=p_sem.at[0, i, dz],
            recv_sem=p_sem.at[1, i, dz],
            device_id=partner,
            device_id_type=MESH,
        )

    def send_z(i):
        def go(core):
            for dz in (1, 7, 2, 6):
                z_send(i, dz, core).start()

        by_core(go)

    def pass_line(i, s):
        def go(core):
            dz = ORDER[s]
            if s:
                z_arrival(i, dz, core).wait_recv()
            for later in ((3, 4) if core == 0 else (3,)) if dz == 2 else ():
                z_send(i, later, core).start()
            for later in ((5,) if core == 0 else (5, 4)) if dz == 6 else ():
                z_send(i, later, core).start()
            for d in (2, 1, 3):
                third_copy(i, dz, d, 0, core).start()

        by_core(go)

    def pass_plane(i, s):
        def go(core):
            dz = ORDER[s]
            for d in (1, 3, 2):
                third_copy(i, dz, d, d, core).wait_recv()

        by_core(go)
        across(i, ORDER[s], g).start()

    def wait_plane(i, s):
        across(i, ORDER[s], 1 - g).wait_recv()

    def finish_sends(i):
        def go(core):
            for dz in ORDER:
                if dz:
                    z_send(i, dz, core).wait_send()
                for d in range(1, NS):
                    third_copy(i, dz, d, 0, core).wait_send()

        by_core(go)
        for dz in ORDER:
            across(i, dz, g).wait_send()

    def prepare():
        for k in range(count // LANES):
            rows_k = slice(k * LANES, (k + 1) * LANES)
            table = tab[rows_k, :]
            cb16[rows_k, :] = table.astype(jnp.bfloat16)
            q = jnp.sum(table * table, axis=1, keepdims=True) * (SHARP * LOG2E)
            qb[rows_k, :] = jnp.broadcast_to(q, (LANES, LANES))

    def tile_dot(i, s, t=None):
        t = wrap(z - ORDER[s], NZ) if t is None else t
        tile = xbs[i][t].reshape(NX * NY * 16, D)
        sbs[s % 2][...] = lax.dot_general(
            cb16[...], tile, (((1,), (1,)), ((), ())), preferred_element_type=jnp.float32
        )

    def tile_soft(i, s, t=None):
        t = wrap(z - ORDER[s], NZ) if t is None else t
        for h in range(2):
            cut = slice(h * LANES, (h + 1) * LANES)
            score = sbs[s % 2][:, cut] * (2.0 * SHARP * LOG2E) - qb[...]
            top = jnp.max(score, axis=0, keepdims=True)
            e = jnp.exp2(score - top)
            total = jnp.sum(e, axis=0, keepdims=True)
            ebuf[2 * t + h] = e
            mbuf[pl.ds(2 * t + h, 1), :] = top
            lbuf[i, pl.ds(2 * t + h, 1), :] = top + jnp.log2(total)

    def merge(parts):
        top = parts[0]
        for part in parts[1:]:
            top = jnp.maximum(top, part)
        total = jnp.exp2(parts[0] - top)
        for part in parts[1:]:
            total = total + jnp.exp2(part - top)
        return top + jnp.log2(total)

    def role(h):
        return g if h == 0 else 1 - g

    def stat_one(i, d, h):
        r = role(h)
        return pltpu.make_async_remote_copy(
            src_ref=lbuf.at[i, pl.ds(8 * h, 8)],
            dst_ref=st1.at[i, d, r],
            send_sem=a_sem.at[0, i, d, r],
            recv_sem=a_sem.at[1, i, d, r],
            device_id=device(wrap(z + d, NZ), x, y, h),
            device_id_type=MESH,
        )

    def stat_arrival(i, d, r):
        return pltpu.make_async_remote_copy(
            src_ref=lbuf.at[i, pl.ds(0, 8)],
            dst_ref=st1.at[i, d, r],
            send_sem=a_sem.at[0, i, d, r],
            recv_sem=a_sem.at[1, i, d, r],
            device_id=partner,
            device_id_type=MESH,
        )

    def stat_two(i, dx, dy, r):
        gg = g if r == 0 else 1 - g
        return pltpu.make_async_remote_copy(
            src_ref=merged.at[i],
            dst_ref=st2.at[i, dx, dy, r],
            send_sem=b_sem.at[0, i, dx, dy, r],
            recv_sem=b_sem.at[1, i, dx, dy, r],
            device_id=device(z, wrap(x + dx, NX), wrap(y + dy, NY), gg),
            device_id_type=MESH,
        )

    def stat_result(i, dx, dy, h):
        r = role(h)
        return pltpu.make_async_remote_copy(
            src_ref=merged.at[i],
            dst_ref=st2.at[i, dx, dy, r],
            send_sem=b_sem.at[0, i, dx, dy, r],
            recv_sem=b_sem.at[1, i, dx, dy, r],
            device_id=partner,
            device_id_type=MESH,
        )

    far = sorted(
        [(dx, dy) for dx in range(NX) for dy in range(NY)],
        key=lambda v: -(min(v[0], NX - v[0]) + min(v[1], NY - v[1])),
    )
    ones = [(d, r) for d in (4, 3, 5, 2, 6, 1, 7, 0) for r in range(2) if d or r]
    twos = [(dx, dy, r) for dx, dy in far for r in range(2) if dx or dy or r]

    def send_stats(i, h):
        for d in (4, 3, 5, 2, 6, 1, 7):
            stat_one(i, d, h).start()

        @pl.when(g == h)
        def _():
            st1[i, 0, 0] = lbuf[i, 8 * h : 8 * h + 8, :]

        @pl.when(g != h)
        def _():
            stat_one(i, 0, h).start()

    def spread_stats(i):
        for d, r in reversed(ones):
            stat_arrival(i, d, r).wait_recv()
        total = merge([st1[i, d, r] for d in range(NZ) for r in range(2)])
        merged[i] = total
        for dx, dy, r in twos:
            stat_two(i, dx, dy, r).start()
        st2[i, 0, 0, 0] = total

    def take_stats(i, h):
        @pl.when(g != h)
        def _():
            stat_result(i, 0, 0, h).wait_recv()

        for dx, dy in reversed(far[:-1]):
            stat_result(i, dx, dy, h).wait_recv()

        r = role(h)
        final = merge([st2[i, dx, dy, r] for dx, dy in far])
        fin[i, 8 * h : 8 * h + 8, :] = final
        return final

    def finish_stats(i):
        for d, r in ones:
            stat_arrival(i, d, r).wait_send()
        for dx, dy, r in twos:
            stat_two(i, dx, dy, r).wait_send()

    def reseeding(i):
        def look(j, carry):
            place, row = carry
            here = ids[i, j] - cent * (2 * count)
            inside = (here >= 0) & (here < 2 * count)
            pick = ids[2 * ITERS + i, j] * 1024 + ids[ITERS + i, j]
            return place + jnp.where(inside, here, 0), row + jnp.where(inside, pick, 0)

        place, row = lax.fori_loop(0, ids.shape[1], look, (jnp.int32(0), jnp.int32(0)))
        group = lax.div(row, 1024)
        inner = lax.rem(row, 1024)
        return place - base, group, inner

    def picked_row(i, group, inner):
        c = lax.div(inner, 8)
        block = xbs[i][lax.div(c, NX * NY), lax.rem(lax.div(c, NY), NX), lax.rem(c, NY)]
        which = lax.broadcasted_iota(jnp.int32, (16, D), 0) == group * 8 + lax.rem(inner, 8)
        return jnp.sum(jnp.where(which, block.astype(jnp.float32), 0.0), axis=0, keepdims=True)

    def update(i, h, final, picked, place, done):
        fac = jnp.exp2(mbuf[8 * h : 8 * h + 8, :] - final)
        rows = NZ * NX * NY * 8
        xhalf = xbs[i].at[pl.ds(h * (NZ // 2), NZ // 2)].reshape(rows, D)
        for k, (at, size) in enumerate(PARTS):
            rows_k = slice(at, at + size)
            part = jnp.zeros((size, LANES), jnp.float32)
            for t in range(NZ):
                w = (ebuf[8 * h + t, rows_k, :] * fac[t : t + 1, :]).astype(jnp.bfloat16)
                wbuf[rows_k, h * rows + t * LANES : h * rows + (t + 1) * LANES] = w
                part = part + w.astype(jnp.float32)
            total = jnp.dot(
                wbuf[rows_k, h * rows : (h + 1) * rows], xhalf[...], preferred_element_type=jnp.float32
            )
            if h == 0:
                tally[rows_k, :] = part
                sums[rows_k, :] = total
                continue
            counts = jnp.sum(tally[rows_k, :] + part, axis=1, keepdims=True)
            table = tab[rows_k, :]
            table = table + (sums[rows_k, :] + total - counts * table) * (1.0 / (counts + 0.05))
            spot = lax.broadcasted_iota(jnp.int32, (size, D), 0) + at
            tab[rows_k, :] = jnp.where(spot == place, picked, table)
            done(k)

    def write_energy(i):
        offset = (x * NY + y) * 16 + g * 8
        row = fin[i, pl.ds(2 * z + lax.div(offset, LANES), 1), :]
        row = pltpu.roll(row, wrap(-lax.rem(offset, LANES), LANES), 1)
        energy[i] = row[:, :8] * (1.0 / (LOG2E * SHARP * D))

    def results(k):
        at, size = PARTS[k]
        part = out.at[pl.ds(pl.multiple_of(base + at, LANES), size)]
        mine = tab.at[pl.ds(at, size)]
        keep = pltpu.make_async_copy(mine, part, o_sem.at[0, k])
        give = pltpu.make_async_remote_copy(
            src_ref=mine,
            dst_ref=part,
            send_sem=o_sem.at[1, k],
            recv_sem=o_sem.at[2, k],
            device_id=partner,
            device_id_type=MESH,
        )
        return keep, give

    def send_result(k):
        for copy in results(k):
            copy.start()

    place_line()
    send_z(0)
    pass_line(0, 0)
    pass_line(1, 0)
    loads[2].wait()
    prepare()
    for s in range(1, NZ + LAG3 + LAGP + 1):
        if s < NZ:
            pass_line(0, s)
        if 0 <= s - LAG3 < NZ:
            pass_plane(0, s - LAG3)
        if s == 5:
            send_z(1)
        if 8 <= s < 12:
            pass_line(1, s - 7)
        done = s - LAG3 - LAGP
        if 0 <= done < NZ:
            wait_plane(0, done)
            tile_dot(0, done)
        if 0 <= done - 1:
            tile_soft(0, done - 1)

    send_stats(0, 0)
    send_stats(0, 1)
    loads[1].wait()
    place, group, inner = reseeding(0)
    for s in range(5, NZ):
        pass_line(1, s)
    for s in range(4):
        pass_plane(1, s)
    spread_stats(0)
    for s in range(4, NZ):
        pass_plane(1, s)
    picked = picked_row(0, group, inner)
    for h in range(2):
        update(0, h, take_stats(0, h), picked, place, lambda k: None)
    prepare()

    for s in range(NZ):
        wait_plane(1, s)
    for t in range(NZ + 1):
        if t < NZ:
            tile_dot(1, t, t)
        if t:
            tile_soft(1, t - 1, t - 1)
        if t == NZ // 2:
            send_stats(1, 0)
    send_stats(1, 1)
    place, group, inner = reseeding(1)
    picked = picked_row(1, group, inner)
    spread_stats(1)
    for h in range(2):
        update(1, h, take_stats(1, h), picked, place, send_result)

    write_energy(0)
    write_energy(1)
    for d, h in firsts:
        first_copy(d, h).wait_send()
    for i in range(ITERS):
        finish_sends(i)
        finish_stats(i)
    for k in range(len(PARTS)):
        keep, give = results(k)
        keep.wait()
        give.wait()


def shards(codebook, batch, dead_ids, reseed_rows, source_group):
    ids = jnp.concatenate([dead_ids, reseed_rows, source_group], axis=0)
    held = codebook.shape[0]
    count = held // 2
    anywhere = pl.BlockSpec(memory_space=pl.ANY)
    rows = NZ * NX * NY * 16
    dma = pltpu.SemaphoreType.DMA
    vmem = pltpu.VMEM
    table, energies = pl.pallas_call(
        kernel,
        out_shape=(
            jax.ShapeDtypeStruct((held, D), jnp.float32),
            jax.ShapeDtypeStruct((ITERS, 1, 8), jnp.float32),
        ),
        in_specs=[pl.BlockSpec(memory_space=pltpu.HBM)] * 3,
        out_specs=(anywhere, pl.BlockSpec(memory_space=vmem)),
        scratch_shapes=[
            vmem((NZ, NX, NY, 16, D), jnp.bfloat16),
            vmem((NZ, NX, NY, 16, D), jnp.bfloat16),
            vmem(batch.shape, batch.dtype),
            pltpu.SMEM(ids.shape, ids.dtype),
            vmem((16, D), jnp.bfloat16),
            vmem((NS, 2, 16, HALF), jnp.bfloat16),
            vmem((count, D), jnp.float32),
            vmem((count, D), jnp.bfloat16),
            vmem((count, LANES), jnp.float32),
            vmem((count, 2 * LANES), jnp.float32),
            vmem((count, 2 * LANES), jnp.float32),
            vmem((2 * NZ, count, LANES), jnp.float32),
            vmem((count, rows), jnp.bfloat16),
            vmem((count, D), jnp.float32),
            vmem((count, LANES), jnp.float32),
            vmem((2 * NZ, LANES), jnp.float32),
            vmem((ITERS, 2 * NZ, LANES), jnp.float32),
            vmem((ITERS, 2 * NZ, LANES), jnp.float32),
            vmem((ITERS, 8, LANES), jnp.float32),
            vmem((ITERS, NZ, 2, 8, LANES), jnp.float32),
            vmem((ITERS, NX, NY, 2, 8, LANES), jnp.float32),
            dma((3,)),
            dma((2, NS, 2)),
            dma((2, ITERS, NZ)),
            dma((2, ITERS, NZ, NS)),
            dma((2, ITERS, NZ)),
            dma((2, ITERS, NZ, 2)),
            dma((2, ITERS, NX, NY, 2)),
            dma((3, len(PARTS))),
        ],
        compiler_params=pltpu.CompilerParams(
            collective_id=0, has_side_effects=True, vmem_limit_bytes=48 * 2**20
        ),
        name="soft_kmeans",
    )(codebook, batch, ids)
    return (table, energies)


def solution(mesh):
    return jax.shard_map(
        shards,
        mesh=mesh,
        in_specs=(P("cent", None), P(None, "rows", "cent", None), P(), P(), P()),
        out_specs=(P("cent", None), P(None, "rows", "cent")),
        check_vma=False,
    )
```

```python
import math

import jax
import jax.numpy as jnp
from jax import lax
from jax.experimental import pallas as pl
from jax.experimental.pallas import tpu as pltpu
from jax.sharding import PartitionSpec as P

D = 768
ITERS = 2
NZ, NX, NY = 8, 4, 4
NS = 4
HALF = D // 2
SHARP = 5.0 / math.sqrt(D)
LOG2E = 1.0 / math.log(2.0)
MESH = pl.DeviceIdType.MESH
LANES = 128
PARTS = ((0, 256), (256, 256))
ORDER = (0, 1, 7, 2, 6, 3, 5, 4)
LAG3, LAGP = 4, 2


def wrap(value, size):
    return lax.rem(value + size, size)


def kernel(
    book,
    batch_in,
    ids_in,
    out,
    energy,
    xb0,
    xb1,
    batch,
    ids,
    own16,
    first,
    tab,
    cb16,
    qb,
    sb0,
    sb1,
    ebuf,
    wbuf,
    sums,
    tally,
    other,
    delta,
    theirs,
    mbuf,
    lbuf,
    fin,
    merged,
    st1,
    st2,
    load_sem,
    f_sem,
    z_sem,
    t_sem,
    p_sem,
    a_sem,
    b_sem,
    o_sem,
    w_sem,
):
    cent = lax.axis_index("cent")
    g = lax.axis_index("rows")
    z = lax.div(cent, NX * NY)
    x = lax.rem(lax.div(cent, NY), NX)
    y = lax.rem(cent, NY)
    xbs = (xb0, xb1)
    sbs = (sb0, sb1)
    count = tab.shape[0]
    base = g * count

    def half(core):
        return pl.ds(pl.multiple_of(core * HALF, LANES), HALF)

    def device(zz, xx, yy, gg):
        return (zz * (NX * NY) + xx * NY + yy, gg)

    def along(core, d):
        return wrap(x + (1 - core) * d, NX), wrap(y + core * d, NY)

    partner = device(z, x, y, 1 - g)

    loads = [
        pltpu.make_async_copy(batch_in, batch, load_sem.at[0]),
        pltpu.make_async_copy(ids_in, ids, load_sem.at[1]),
        pltpu.make_async_copy(
            book.at[pl.ds(pl.multiple_of(base, 256), count)], tab, load_sem.at[2]
        ),
    ]
    for load in loads:
        load.start()

    barrier = pltpu.get_barrier_semaphore()

    def greet(to):
        pl.semaphore_signal(barrier, inc=1, device_id=to, device_id_type=MESH)

    for d in (1, 2, NZ - 2, NZ - 1):
        greet(device(wrap(z + d, NZ), x, y, g))
    for d in range(1, NS):
        for gg in (g, 1 - g):
            greet(device(z, wrap(x + d, NX), y, gg))
            greet(device(z, x, wrap(y + d, NY), gg))
    greet(partner)
    loads[0].wait()
    own16[...] = jnp.concatenate(
        [batch[0, 0].astype(jnp.float32), batch[1, 0].astype(jnp.float32)], axis=0
    ).astype(jnp.bfloat16)
    pl.semaphore_wait(barrier, 4 + 4 * (NS - 1) + 1)

    def first_copy(d, h):
        core = g if h == 0 else 1 - g
        xx, yy = along(core, d)
        return pltpu.make_async_remote_copy(
            src_ref=own16.at[:, half(core)],
            dst_ref=first.at[d, h],
            send_sem=f_sem.at[0, d, h],
            recv_sem=f_sem.at[1, d, h],
            device_id=device(z, xx, yy, core),
            device_id_type=MESH,
        )

    firsts = [(d, h) for d in (2, 1, 3, 0) for h in range(2) if d or h]
    for d, h in firsts:
        first_copy(d, h).start()
    first[0, 0] = own16[:, half(g)]

    def place_line():
        for d, h in firsts:
            first_copy(d, h).wait_recv()
        for d in range(NS):
            same = first[d, 0].astype(jnp.float32)
            other = first[d, 1].astype(jnp.float32)
            xx, yy = along(g, -d)
            for i in range(ITERS):
                rows_i = slice(8 * i, 8 * i + 8)
                a = jnp.where(g == 0, same[rows_i], other[rows_i])
                b = jnp.where(g == 0, other[rows_i], same[rows_i])
                block = jnp.concatenate([a, b], axis=0).astype(jnp.bfloat16)
                xbs[i][z, xx, yy, :, half(g)] = block

    def by_core(f):
        pl.when(g == 0)(lambda: f(0))
        pl.when(g == 1)(lambda: f(1))

    def line(i, zz, back, core):
        if core == 0:
            return xbs[i].at[zz, :, wrap(y - back, NY), :, half(0)]
        return xbs[i].at[zz, wrap(x - back, NX), :, :, half(1)]

    def z_step(dz, core):
        if dz == 4:
            return 2 if core == 0 else -2
        return {1: 1, 2: 2, 3: 1, 5: -1, 6: -2, 7: -1}[dz]

    def z_send(i, dz, core):
        step = z_step(dz, core)
        ref = line(i, wrap(z - dz + (step if step > 0 else step + NZ), NZ), 0, core)
        return pltpu.make_async_remote_copy(
            src_ref=ref,
            dst_ref=ref,
            send_sem=z_sem.at[0, i, dz],
            recv_sem=z_sem.at[1, i, dz],
            device_id=device(wrap(z + step, NZ), x, y, core),
            device_id_type=MESH,
        )

    def z_arrival(i, dz, core):
        ref = line(i, wrap(z - dz, NZ), 0, core)
        return pltpu.make_async_remote_copy(
            src_ref=ref,
            dst_ref=ref,
            send_sem=z_sem.at[0, i, dz],
            recv_sem=z_sem.at[1, i, dz],
            device_id=device(wrap(z + z_step(dz, core), NZ), x, y, core),
            device_id_type=MESH,
        )

    def third_copy(i, dz, d, back, core):
        ref = line(i, wrap(z - dz, NZ), back, core)
        xx, yy = (x, wrap(y + d, NY)) if core == 0 else (wrap(x + d, NX), y)
        return pltpu.make_async_remote_copy(
            src_ref=ref,
            dst_ref=ref,
            send_sem=t_sem.at[0, i, dz, d],
            recv_sem=t_sem.at[1, i, dz, d],
            device_id=device(z, xx, yy, core),
            device_id_type=MESH,
        )

    def across(i, dz, core):
        ref = xbs[i].at[wrap(z - dz, NZ), :, :, :, half(core)]
        return pltpu.make_async_remote_copy(
            src_ref=ref,
            dst_ref=ref,
            send_sem=p_sem.at[0, i, dz],
            recv_sem=p_sem.at[1, i, dz],
            device_id=partner,
            device_id_type=MESH,
        )

    def send_z(i):
        def go(core):
            for dz in (1, 7, 2, 6):
                z_send(i, dz, core).start()

        by_core(go)

    def pass_line(i, s):
        def go(core):
            dz = ORDER[s]
            if s:
                z_arrival(i, dz, core).wait_recv()
            for later in ((3, 4) if core == 0 else (3,)) if dz == 2 else ():
                z_send(i, later, core).start()
            for later in ((5,) if core == 0 else (5, 4)) if dz == 6 else ():
                z_send(i, later, core).start()
            for d in (2, 1, 3):
                third_copy(i, dz, d, 0, core).start()

        by_core(go)

    def pass_plane(i, s):
        def go(core):
            dz = ORDER[s]
            for d in (1, 3, 2):
                third_copy(i, dz, d, d, core).wait_recv()

        by_core(go)
        across(i, ORDER[s], g).start()

    def wait_plane(i, s):
        across(i, ORDER[s], 1 - g).wait_recv()

    def finish_sends(i):
        def go(core):
            for dz in ORDER:
                if dz:
                    z_send(i, dz, core).wait_send()
                for d in range(1, NS):
                    third_copy(i, dz, d, 0, core).wait_send()

        by_core(go)
        for dz in ORDER:
            across(i, dz, g).wait_send()

    def prepare():
        for k in range(count // LANES):
            rows_k = slice(k * LANES, (k + 1) * LANES)
            table = tab[rows_k, :]
            cb16[rows_k, :] = table.astype(jnp.bfloat16)
            q = jnp.sum(table * table, axis=1, keepdims=True) * (SHARP * LOG2E)
            qb[rows_k, :] = jnp.broadcast_to(q, (LANES, LANES))

    def tile_dot(i, s, t=None):
        t = wrap(z - ORDER[s], NZ) if t is None else t
        tile = xbs[i][t].reshape(NX * NY * 16, D)
        sbs[s % 2][...] = lax.dot_general(
            cb16[...], tile, (((1,), (1,)), ((), ())), preferred_element_type=jnp.float32
        )

    def tile_soft(i, s, t=None):
        t = wrap(z - ORDER[s], NZ) if t is None else t
        for h in range(2):
            cut = slice(h * LANES, (h + 1) * LANES)
            score = sbs[s % 2][:, cut] * (2.0 * SHARP * LOG2E) - qb[...]
            top = jnp.max(score, axis=0, keepdims=True)
            e = jnp.exp2(score - top)
            total = jnp.sum(e, axis=0, keepdims=True)
            ebuf[2 * t + h] = e
            mbuf[pl.ds(2 * t + h, 1), :] = top
            lbuf[i, pl.ds(2 * t + h, 1), :] = top + jnp.log2(total)

    def merge(parts):
        top = parts[0]
        for part in parts[1:]:
            top = jnp.maximum(top, part)
        total = jnp.exp2(parts[0] - top)
        for part in parts[1:]:
            total = total + jnp.exp2(part - top)
        return top + jnp.log2(total)

    def role(h):
        return g if h == 0 else 1 - g

    def stat_one(i, d, h):
        r = role(h)
        return pltpu.make_async_remote_copy(
            src_ref=lbuf.at[i, pl.ds(8 * h, 8)],
            dst_ref=st1.at[i, d, r],
            send_sem=a_sem.at[0, i, d, r],
            recv_sem=a_sem.at[1, i, d, r],
            device_id=device(wrap(z + d, NZ), x, y, h),
            device_id_type=MESH,
        )

    def stat_arrival(i, d, r):
        return pltpu.make_async_remote_copy(
            src_ref=lbuf.at[i, pl.ds(0, 8)],
            dst_ref=st1.at[i, d, r],
            send_sem=a_sem.at[0, i, d, r],
            recv_sem=a_sem.at[1, i, d, r],
            device_id=partner,
            device_id_type=MESH,
        )

    def stat_two(i, dx, dy, r):
        gg = g if r == 0 else 1 - g
        return pltpu.make_async_remote_copy(
            src_ref=merged.at[i],
            dst_ref=st2.at[i, dx, dy, r],
            send_sem=b_sem.at[0, i, dx, dy, r],
            recv_sem=b_sem.at[1, i, dx, dy, r],
            device_id=device(z, wrap(x + dx, NX), wrap(y + dy, NY), gg),
            device_id_type=MESH,
        )

    def stat_result(i, dx, dy, h):
        r = role(h)
        return pltpu.make_async_remote_copy(
            src_ref=merged.at[i],
            dst_ref=st2.at[i, dx, dy, r],
            send_sem=b_sem.at[0, i, dx, dy, r],
            recv_sem=b_sem.at[1, i, dx, dy, r],
            device_id=partner,
            device_id_type=MESH,
        )

    far = sorted(
        [(dx, dy) for dx in range(NX) for dy in range(NY)],
        key=lambda v: -(min(v[0], NX - v[0]) + min(v[1], NY - v[1])),
    )
    ones = [(d, r) for d in (4, 3, 5, 2, 6, 1, 7, 0) for r in range(2) if d or r]
    twos = [(dx, dy, r) for dx, dy in far for r in range(2) if dx or dy or r]

    def send_stats(i, h):
        for d in (4, 3, 5, 2, 6, 1, 7):
            stat_one(i, d, h).start()

        @pl.when(g == h)
        def _():
            st1[i, 0, 0] = lbuf[i, 8 * h : 8 * h + 8, :]

        @pl.when(g != h)
        def _():
            stat_one(i, 0, h).start()

    def spread_stats(i):
        for d, r in reversed(ones):
            stat_arrival(i, d, r).wait_recv()
        total = merge([st1[i, d, r] for d in range(NZ) for r in range(2)])
        merged[i] = total
        for dx, dy, r in twos:
            stat_two(i, dx, dy, r).start()
        st2[i, 0, 0, 0] = total

    def take_stats(i, h):
        @pl.when(g != h)
        def _():
            stat_result(i, 0, 0, h).wait_recv()

        for dx, dy in reversed(far[:-1]):
            stat_result(i, dx, dy, h).wait_recv()

        r = role(h)
        final = merge([st2[i, dx, dy, r] for dx, dy in far])
        fin[i, 8 * h : 8 * h + 8, :] = final
        return final

    def finish_stats(i):
        for d, r in ones:
            stat_arrival(i, d, r).wait_send()
        for dx, dy, r in twos:
            stat_two(i, dx, dy, r).wait_send()

    def reseeding(i):
        def look(j, carry):
            place, row = carry
            here = ids[i, j] - cent * (2 * count)
            inside = (here >= 0) & (here < 2 * count)
            pick = ids[2 * ITERS + i, j] * 1024 + ids[ITERS + i, j]
            return place + jnp.where(inside, here, 0), row + jnp.where(inside, pick, 0)

        place, row = lax.fori_loop(0, ids.shape[1], look, (jnp.int32(0), jnp.int32(0)))
        group = lax.div(row, 1024)
        inner = lax.rem(row, 1024)
        return place - base, group, inner

    def picked_row(i, group, inner):
        c = lax.div(inner, 8)
        block = xbs[i][lax.div(c, NX * NY), lax.rem(lax.div(c, NY), NX), lax.rem(c, NY)]
        which = lax.broadcasted_iota(jnp.int32, (16, D), 0) == group * 8 + lax.rem(inner, 8)
        return jnp.sum(jnp.where(which, block.astype(jnp.float32), 0.0), axis=0, keepdims=True)

    def update(i, h, final, picked, place, done):
        fac = jnp.exp2(mbuf[8 * h : 8 * h + 8, :] - final)
        rows = NZ * NX * NY * 8
        xhalf = xbs[i].at[pl.ds(h * (NZ // 2), NZ // 2)].reshape(rows, D)
        for k, (at, size) in enumerate(PARTS):
            rows_k = slice(at, at + size)
            part = jnp.zeros((size, LANES), jnp.float32)
            for t in range(NZ):
                w = (ebuf[8 * h + t, rows_k, :] * fac[t : t + 1, :]).astype(jnp.bfloat16)
                wbuf[rows_k, h * rows + t * LANES : h * rows + (t + 1) * LANES] = w
                part = part + w.astype(jnp.float32)
            total = jnp.dot(
                wbuf[rows_k, h * rows : (h + 1) * rows], xhalf[...], preferred_element_type=jnp.float32
            )
            if h == 0:
                tally[rows_k, :] = part
                sums[rows_k, :] = total
                continue
            counts = jnp.sum(tally[rows_k, :] + part, axis=1, keepdims=True)
            table = tab[rows_k, :]
            change = (sums[rows_k, :] + total - counts * table) * (1.0 / (counts + 0.05))
            if i == ITERS - 1:
                delta[rows_k, :] = change.astype(jnp.bfloat16)
                change = delta[rows_k, :].astype(jnp.float32)
            table = table + change
            spot = lax.broadcasted_iota(jnp.int32, (size, D), 0) + at
            tab[rows_k, :] = jnp.where(spot == place, picked, table)
            done(k)

    def write_energy(i):
        offset = (x * NY + y) * 16 + g * 8
        row = fin[i, pl.ds(2 * z + lax.div(offset, LANES), 1), :]
        row = pltpu.roll(row, wrap(-lax.rem(offset, LANES), LANES), 1)
        energy[i] = row[:, :8] * (1.0 / (LOG2E * SHARP * D))

    def results(k):
        at, size = PARTS[k]
        part = out.at[pl.ds(pl.multiple_of(base + at, LANES), size)]
        mine = tab.at[pl.ds(at, size)]
        keep = pltpu.make_async_copy(mine, part, o_sem.at[0, k])
        give = pltpu.make_async_remote_copy(
            src_ref=delta.at[pl.ds(at, size)],
            dst_ref=theirs.at[pl.ds(at, size)],
            send_sem=o_sem.at[1, k],
            recv_sem=o_sem.at[2, k],
            device_id=partner,
            device_id_type=MESH,
        )
        return keep, give

    def put(k):
        at, size = PARTS[k]
        part = out.at[pl.ds(pl.multiple_of((1 - g) * count + at, LANES), size)]
        return pltpu.make_async_copy(other.at[pl.ds(at, size)], part, o_sem.at[3, k])

    ship = pltpu.make_async_remote_copy(
        src_ref=tab,
        dst_ref=other,
        send_sem=w_sem.at[0],
        recv_sem=w_sem.at[1],
        device_id=partner,
        device_id_type=MESH,
    )

    def send_result(k):
        for copy in results(k):
            copy.start()

    place_line()
    send_z(0)
    pass_line(0, 0)
    pass_line(1, 0)
    loads[2].wait()
    prepare()
    for s in range(1, NZ + LAG3 + LAGP + 1):
        if s < NZ:
            pass_line(0, s)
        if 0 <= s - LAG3 < NZ:
            pass_plane(0, s - LAG3)
        if s == 5:
            send_z(1)
        if 8 <= s < 12:
            pass_line(1, s - 7)
        done = s - LAG3 - LAGP
        if 0 <= done < NZ:
            wait_plane(0, done)
            tile_dot(0, done)
        if 0 <= done - 1:
            tile_soft(0, done - 1)

    send_stats(0, 0)
    send_stats(0, 1)
    loads[1].wait()
    place, group, inner = reseeding(0)
    for s in range(5, NZ):
        pass_line(1, s)
    for s in range(4):
        pass_plane(1, s)
    spread_stats(0)
    for s in range(4, NZ):
        pass_plane(1, s)
    picked = picked_row(0, group, inner)
    for h in range(2):
        update(0, h, take_stats(0, h), picked, place, lambda k: None)
    prepare()

    for s in range(NZ):
        wait_plane(1, s)
    ship.start()
    for t in range(NZ + 1):
        if t < NZ:
            tile_dot(1, t, t)
        if t:
            tile_soft(1, t - 1, t - 1)
        if t == NZ // 2:
            send_stats(1, 0)
    send_stats(1, 1)
    place, group, inner = reseeding(1)
    picked = picked_row(1, group, inner)
    for d, h in firsts:
        first_copy(d, h).wait_send()
    for i in range(ITERS):
        finish_sends(i)
    finish_stats(0)
    write_energy(0)
    spread_stats(1)
    ship.wait()
    for h in range(2):
        update(1, h, take_stats(1, h), picked, place, send_result)

    write_energy(1)
    their_place = place + (2 * g - 1) * count
    for k, (at, size) in enumerate(PARTS):
        keep, give = results(k)
        give.wait_recv()
        rows_k = slice(at, at + size)
        spot = lax.broadcasted_iota(jnp.int32, (size, D), 0) + at
        table = other[rows_k, :] + theirs[rows_k, :].astype(jnp.float32)
        other[rows_k, :] = jnp.where(spot == their_place, picked, table)
        put(k).start()
    finish_stats(1)
    for k in range(len(PARTS)):
        keep, give = results(k)
        keep.wait()
        give.wait_send()
        put(k).wait()


def shards(codebook, batch, dead_ids, reseed_rows, source_group):
    ids = jnp.concatenate([dead_ids, reseed_rows, source_group], axis=0)
    held = codebook.shape[0]
    count = held // 2
    anywhere = pl.BlockSpec(memory_space=pl.ANY)
    rows = NZ * NX * NY * 16
    dma = pltpu.SemaphoreType.DMA
    vmem = pltpu.VMEM
    table, energies = pl.pallas_call(
        kernel,
        out_shape=(
            jax.ShapeDtypeStruct((held, D), jnp.float32),
            jax.ShapeDtypeStruct((ITERS, 1, 8), jnp.float32),
        ),
        in_specs=[pl.BlockSpec(memory_space=pltpu.HBM)] * 3,
        out_specs=(anywhere, pl.BlockSpec(memory_space=vmem)),
        scratch_shapes=[
            vmem((NZ, NX, NY, 16, D), jnp.bfloat16),
            vmem((NZ, NX, NY, 16, D), jnp.bfloat16),
            vmem(batch.shape, batch.dtype),
            pltpu.SMEM(ids.shape, ids.dtype),
            vmem((16, D), jnp.bfloat16),
            vmem((NS, 2, 16, HALF), jnp.bfloat16),
            vmem((count, D), jnp.float32),
            vmem((count, D), jnp.bfloat16),
            vmem((count, LANES), jnp.float32),
            vmem((count, 2 * LANES), jnp.float32),
            vmem((count, 2 * LANES), jnp.float32),
            vmem((2 * NZ, count, LANES), jnp.float32),
            vmem((count, rows), jnp.bfloat16),
            vmem((count, D), jnp.float32),
            vmem((count, LANES), jnp.float32),
            vmem((count, D), jnp.float32),
            vmem((count, D), jnp.bfloat16),
            vmem((count, D), jnp.bfloat16),
            vmem((2 * NZ, LANES), jnp.float32),
            vmem((ITERS, 2 * NZ, LANES), jnp.float32),
            vmem((ITERS, 2 * NZ, LANES), jnp.float32),
            vmem((ITERS, 8, LANES), jnp.float32),
            vmem((ITERS, NZ, 2, 8, LANES), jnp.float32),
            vmem((ITERS, NX, NY, 2, 8, LANES), jnp.float32),
            dma((3,)),
            dma((2, NS, 2)),
            dma((2, ITERS, NZ)),
            dma((2, ITERS, NZ, NS)),
            dma((2, ITERS, NZ)),
            dma((2, ITERS, NZ, 2)),
            dma((2, ITERS, NX, NY, 2)),
            dma((4, len(PARTS))),
            dma((2,)),
        ],
        compiler_params=pltpu.CompilerParams(
            collective_id=0, has_side_effects=True, vmem_limit_bytes=48 * 2**20
        ),
        name="soft_kmeans",
    )(codebook, batch, ids)
    return (table, energies)


def solution(mesh):
    return jax.shard_map(
        shards,
        mesh=mesh,
        in_specs=(P("cent", None), P(None, "rows", "cent", None), P(), P(), P()),
        out_specs=(P("cent", None), P(None, "rows", "cent")),
        check_vma=False,
    )
```

```python
import math

import jax
import jax.numpy as jnp
from jax import lax
from jax.experimental import pallas as pl
from jax.experimental.pallas import tpu as pltpu
from jax.sharding import PartitionSpec as P

D = 768
ITERS = 2
NZ, NX, NY = 8, 4, 4
NS = 4
HALF = D // 2
SHARP = 5.0 / math.sqrt(D)
LOG2E = 1.0 / math.log(2.0)
MESH = pl.DeviceIdType.MESH
LANES = 128
PARTS = ((0, 256), (256, 256))
ORDER = (0, 1, 7, 2, 6, 3, 5, 4)
LAG3, LAGP = 4, 2


def wrap(value, size):
    return lax.rem(value + size, size)


def kernel(
    book,
    batch_in,
    ids_in,
    out,
    energy,
    xb0,
    xb1,
    batch,
    ids,
    own16,
    first,
    tab,
    cb16,
    qb,
    sb0,
    sb1,
    ebuf,
    wbuf,
    sums,
    tally,
    other,
    delta,
    theirs,
    mbuf,
    lbuf,
    fin,
    merged,
    st1,
    st2,
    load_sem,
    f_sem,
    z_sem,
    t_sem,
    p_sem,
    a_sem,
    b_sem,
    o_sem,
    w_sem,
):
    cent = lax.axis_index("cent")
    g = lax.axis_index("rows")
    z = lax.div(cent, NX * NY)
    x = lax.rem(lax.div(cent, NY), NX)
    y = lax.rem(cent, NY)
    xbs = (xb0, xb1)
    sbs = (sb0, sb1)
    count = tab.shape[0]
    base = g * count

    def half(core):
        return pl.ds(pl.multiple_of(core * HALF, LANES), HALF)

    def device(zz, xx, yy, gg):
        return (zz * (NX * NY) + xx * NY + yy, gg)

    def along(core, d):
        return wrap(x + (1 - core) * d, NX), wrap(y + core * d, NY)

    partner = device(z, x, y, 1 - g)

    loads = [
        pltpu.make_async_copy(batch_in, batch, load_sem.at[0]),
        pltpu.make_async_copy(ids_in, ids, load_sem.at[1]),
        pltpu.make_async_copy(
            book.at[pl.ds(pl.multiple_of(base, 256), count)], tab, load_sem.at[2]
        ),
    ]
    for load in loads:
        load.start()

    barrier = pltpu.get_barrier_semaphore()

    def greet(to):
        pl.semaphore_signal(barrier, inc=1, device_id=to, device_id_type=MESH)

    for d in (1, 2, NZ - 2, NZ - 1):
        greet(device(wrap(z + d, NZ), x, y, g))
    for d in range(1, NS):
        for gg in (g, 1 - g):
            greet(device(z, wrap(x + d, NX), y, gg))
            greet(device(z, x, wrap(y + d, NY), gg))
    greet(partner)
    loads[0].wait()
    own16[...] = jnp.concatenate(
        [batch[0, 0].astype(jnp.float32), batch[1, 0].astype(jnp.float32)], axis=0
    ).astype(jnp.bfloat16)
    pl.semaphore_wait(barrier, 4 + 4 * (NS - 1) + 1)

    def first_copy(d, h):
        core = g if h == 0 else 1 - g
        xx, yy = along(core, d)
        return pltpu.make_async_remote_copy(
            src_ref=own16.at[:, half(core)],
            dst_ref=first.at[d, h],
            send_sem=f_sem.at[0, d, h],
            recv_sem=f_sem.at[1, d, h],
            device_id=device(z, xx, yy, core),
            device_id_type=MESH,
        )

    firsts = [(d, h) for d in (2, 1, 3, 0) for h in range(2) if d or h]
    for d, h in firsts:
        first_copy(d, h).start()
    first[0, 0] = own16[:, half(g)]

    def place_line():
        for d, h in firsts:
            first_copy(d, h).wait_recv()
        for d in range(NS):
            same = first[d, 0].astype(jnp.float32)
            other = first[d, 1].astype(jnp.float32)
            xx, yy = along(g, -d)
            for i in range(ITERS):
                rows_i = slice(8 * i, 8 * i + 8)
                a = jnp.where(g == 0, same[rows_i], other[rows_i])
                b = jnp.where(g == 0, other[rows_i], same[rows_i])
                block = jnp.concatenate([a, b], axis=0).astype(jnp.bfloat16)
                xbs[i][z, xx, yy, :, half(g)] = block

    def by_core(f):
        pl.when(g == 0)(lambda: f(0))
        pl.when(g == 1)(lambda: f(1))

    def line(i, zz, back, core):
        if core == 0:
            return xbs[i].at[zz, :, wrap(y - back, NY), :, half(0)]
        return xbs[i].at[zz, wrap(x - back, NX), :, :, half(1)]

    def z_step(dz, core):
        if dz == 4:
            return 2 if core == 0 else -2
        return {1: 1, 2: 2, 3: 1, 5: -1, 6: -2, 7: -1}[dz]

    def z_send(i, dz, core):
        step = z_step(dz, core)
        ref = line(i, wrap(z - dz + (step if step > 0 else step + NZ), NZ), 0, core)
        return pltpu.make_async_remote_copy(
            src_ref=ref,
            dst_ref=ref,
            send_sem=z_sem.at[0, i, dz],
            recv_sem=z_sem.at[1, i, dz],
            device_id=device(wrap(z + step, NZ), x, y, core),
            device_id_type=MESH,
        )

    def z_arrival(i, dz, core):
        ref = line(i, wrap(z - dz, NZ), 0, core)
        return pltpu.make_async_remote_copy(
            src_ref=ref,
            dst_ref=ref,
            send_sem=z_sem.at[0, i, dz],
            recv_sem=z_sem.at[1, i, dz],
            device_id=device(wrap(z + z_step(dz, core), NZ), x, y, core),
            device_id_type=MESH,
        )

    def third_copy(i, dz, d, back, core):
        ref = line(i, wrap(z - dz, NZ), back, core)
        xx, yy = (x, wrap(y + d, NY)) if core == 0 else (wrap(x + d, NX), y)
        return pltpu.make_async_remote_copy(
            src_ref=ref,
            dst_ref=ref,
            send_sem=t_sem.at[0, i, dz, d],
            recv_sem=t_sem.at[1, i, dz, d],
            device_id=device(z, xx, yy, core),
            device_id_type=MESH,
        )

    def across(i, dz, core):
        ref = xbs[i].at[wrap(z - dz, NZ), :, :, :, half(core)]
        return pltpu.make_async_remote_copy(
            src_ref=ref,
            dst_ref=ref,
            send_sem=p_sem.at[0, i, dz],
            recv_sem=p_sem.at[1, i, dz],
            device_id=partner,
            device_id_type=MESH,
        )

    def send_z(i):
        def go(core):
            for dz in (1, 7, 2, 6):
                z_send(i, dz, core).start()

        by_core(go)

    def pass_line(i, s):
        def go(core):
            dz = ORDER[s]
            if s:
                z_arrival(i, dz, core).wait_recv()
            for later in ((3, 4) if core == 0 else (3,)) if dz == 2 else ():
                z_send(i, later, core).start()
            for later in ((5,) if core == 0 else (5, 4)) if dz == 6 else ():
                z_send(i, later, core).start()
            for d in (2, 1, 3):
                third_copy(i, dz, d, 0, core).start()

        by_core(go)

    def pass_plane(i, s):
        def go(core):
            dz = ORDER[s]
            for d in (1, 3, 2):
                third_copy(i, dz, d, d, core).wait_recv()

        by_core(go)
        across(i, ORDER[s], g).start()

    def wait_plane(i, s):
        across(i, ORDER[s], 1 - g).wait_recv()

    def finish_sends(i):
        def go(core):
            for dz in ORDER:
                if dz:
                    z_send(i, dz, core).wait_send()
                for d in range(1, NS):
                    third_copy(i, dz, d, 0, core).wait_send()

        by_core(go)
        for dz in ORDER:
            across(i, dz, g).wait_send()

    def prepare(at, size):
        for k in range(at // LANES, (at + size) // LANES):
            rows_k = slice(k * LANES, (k + 1) * LANES)
            table = tab[rows_k, :]
            cb16[rows_k, :] = table.astype(jnp.bfloat16)
            q = jnp.sum(table * table, axis=1, keepdims=True) * (SHARP * LOG2E)
            qb[rows_k, :] = jnp.broadcast_to(q, (LANES, LANES))

    def tile_dot(i, s, t=None):
        t = wrap(z - ORDER[s], NZ) if t is None else t
        tile = xbs[i][t].reshape(NX * NY * 16, D)
        sbs[s % 2][...] = lax.dot_general(
            cb16[...], tile, (((1,), (1,)), ((), ())), preferred_element_type=jnp.float32
        )

    def tile_soft(i, s, t=None):
        t = wrap(z - ORDER[s], NZ) if t is None else t
        for h in range(2):
            cut = slice(h * LANES, (h + 1) * LANES)
            score = sbs[s % 2][:, cut] * (2.0 * SHARP * LOG2E) - qb[...]
            top = jnp.max(score, axis=0, keepdims=True)
            e = jnp.exp2(score - top)
            total = jnp.sum(e, axis=0, keepdims=True)
            ebuf[2 * t + h] = e
            mbuf[pl.ds(2 * t + h, 1), :] = top
            lbuf[i, pl.ds(2 * t + h, 1), :] = top + jnp.log2(total)

    def merge(parts):
        top = parts[0]
        for part in parts[1:]:
            top = jnp.maximum(top, part)
        total = jnp.exp2(parts[0] - top)
        for part in parts[1:]:
            total = total + jnp.exp2(part - top)
        return top + jnp.log2(total)

    def role(h):
        return g if h == 0 else 1 - g

    def stat_one(i, d, h):
        r = role(h)
        return pltpu.make_async_remote_copy(
            src_ref=lbuf.at[i, pl.ds(8 * h, 8)],
            dst_ref=st1.at[i, d, r],
            send_sem=a_sem.at[0, i, d, r],
            recv_sem=a_sem.at[1, i, d, r],
            device_id=device(wrap(z + d, NZ), x, y, h),
            device_id_type=MESH,
        )

    def stat_arrival(i, d, r):
        return pltpu.make_async_remote_copy(
            src_ref=lbuf.at[i, pl.ds(0, 8)],
            dst_ref=st1.at[i, d, r],
            send_sem=a_sem.at[0, i, d, r],
            recv_sem=a_sem.at[1, i, d, r],
            device_id=partner,
            device_id_type=MESH,
        )

    def stat_two(i, dx, dy, r):
        gg = g if r == 0 else 1 - g
        return pltpu.make_async_remote_copy(
            src_ref=merged.at[i],
            dst_ref=st2.at[i, dx, dy, r],
            send_sem=b_sem.at[0, i, dx, dy, r],
            recv_sem=b_sem.at[1, i, dx, dy, r],
            device_id=device(z, wrap(x + dx, NX), wrap(y + dy, NY), gg),
            device_id_type=MESH,
        )

    def stat_result(i, dx, dy, h):
        r = role(h)
        return pltpu.make_async_remote_copy(
            src_ref=merged.at[i],
            dst_ref=st2.at[i, dx, dy, r],
            send_sem=b_sem.at[0, i, dx, dy, r],
            recv_sem=b_sem.at[1, i, dx, dy, r],
            device_id=partner,
            device_id_type=MESH,
        )

    far = sorted(
        [(dx, dy) for dx in range(NX) for dy in range(NY)],
        key=lambda v: -(min(v[0], NX - v[0]) + min(v[1], NY - v[1])),
    )
    ones = [(d, r) for d in (4, 3, 5, 2, 6, 1, 7, 0) for r in range(2) if d or r]
    twos = [(dx, dy, r) for dx, dy in far for r in range(2) if dx or dy or r]

    def send_stats(i, h):
        for d in (4, 3, 5, 2, 6, 1, 7):
            stat_one(i, d, h).start()

        @pl.when(g == h)
        def _():
            st1[i, 0, 0] = lbuf[i, 8 * h : 8 * h + 8, :]

        @pl.when(g != h)
        def _():
            stat_one(i, 0, h).start()

    def spread_stats(i):
        for d, r in reversed(ones):
            stat_arrival(i, d, r).wait_recv()
        total = merge([st1[i, d, r] for d in range(NZ) for r in range(2)])
        merged[i] = total
        for dx, dy, r in twos:
            stat_two(i, dx, dy, r).start()
        st2[i, 0, 0, 0] = total

    def take_stats(i, h):
        @pl.when(g != h)
        def _():
            stat_result(i, 0, 0, h).wait_recv()

        for dx, dy in reversed(far[:-1]):
            stat_result(i, dx, dy, h).wait_recv()

        r = role(h)
        final = merge([st2[i, dx, dy, r] for dx, dy in far])
        fin[i, 8 * h : 8 * h + 8, :] = final
        return final

    def finish_stats(i):
        for d, r in ones:
            stat_arrival(i, d, r).wait_send()
        for dx, dy, r in twos:
            stat_two(i, dx, dy, r).wait_send()

    def reseeding(i):
        def look(j, carry):
            place, row = carry
            here = ids[i, j] - cent * (2 * count)
            inside = (here >= 0) & (here < 2 * count)
            pick = ids[2 * ITERS + i, j] * 1024 + ids[ITERS + i, j]
            return place + jnp.where(inside, here, 0), row + jnp.where(inside, pick, 0)

        place, row = lax.fori_loop(0, ids.shape[1], look, (jnp.int32(0), jnp.int32(0)))
        group = lax.div(row, 1024)
        inner = lax.rem(row, 1024)
        return place - base, group, inner

    def picked_row(i, group, inner):
        c = lax.div(inner, 8)
        block = xbs[i][lax.div(c, NX * NY), lax.rem(lax.div(c, NY), NX), lax.rem(c, NY)]
        which = lax.broadcasted_iota(jnp.int32, (16, D), 0) == group * 8 + lax.rem(inner, 8)
        return jnp.sum(jnp.where(which, block.astype(jnp.float32), 0.0), axis=0, keepdims=True)

    def update(i, h, final, picked, place, done):
        fac = jnp.exp2(mbuf[8 * h : 8 * h + 8, :] - final)
        rows = NZ * NX * NY * 8
        xhalf = xbs[i].at[pl.ds(h * (NZ // 2), NZ // 2)].reshape(rows, D)
        for k, (at, size) in enumerate(PARTS):
            rows_k = slice(at, at + size)
            part = jnp.zeros((size, LANES), jnp.float32)
            for t in range(NZ):
                w = (ebuf[8 * h + t, rows_k, :] * fac[t : t + 1, :]).astype(jnp.bfloat16)
                wbuf[rows_k, h * rows + t * LANES : h * rows + (t + 1) * LANES] = w
                part = part + w.astype(jnp.float32)
            total = jnp.dot(
                wbuf[rows_k, h * rows : (h + 1) * rows], xhalf[...], preferred_element_type=jnp.float32
            )
            if h == 0:
                tally[rows_k, :] = part
                sums[rows_k, :] = total
                continue
            counts = jnp.sum(tally[rows_k, :] + part, axis=1, keepdims=True)
            table = tab[rows_k, :]
            change = (sums[rows_k, :] + total - counts * table) * (1.0 / (counts + 0.05))
            if i == ITERS - 1:
                delta[rows_k, :] = change.astype(jnp.bfloat16)
                change = delta[rows_k, :].astype(jnp.float32)
            table = table + change
            spot = lax.broadcasted_iota(jnp.int32, (size, D), 0) + at
            tab[rows_k, :] = jnp.where(spot == place, picked, table)
            done(k)

    def write_energy(i):
        offset = (x * NY + y) * 16 + g * 8
        row = fin[i, pl.ds(2 * z + lax.div(offset, LANES), 1), :]
        row = pltpu.roll(row, wrap(-lax.rem(offset, LANES), LANES), 1)
        energy[i] = row[:, :8] * (1.0 / (LOG2E * SHARP * D))

    def results(k):
        at, size = PARTS[k]
        part = out.at[pl.ds(pl.multiple_of(base + at, LANES), size)]
        mine = tab.at[pl.ds(at, size)]
        keep = pltpu.make_async_copy(mine, part, o_sem.at[0, k])
        give = pltpu.make_async_remote_copy(
            src_ref=delta.at[pl.ds(at, size)],
            dst_ref=theirs.at[pl.ds(at, size)],
            send_sem=o_sem.at[1, k],
            recv_sem=o_sem.at[2, k],
            device_id=partner,
            device_id_type=MESH,
        )
        return keep, give

    def put(k):
        at, size = PARTS[k]
        part = out.at[pl.ds(pl.multiple_of((1 - g) * count + at, LANES), size)]
        return pltpu.make_async_copy(other.at[pl.ds(at, size)], part, o_sem.at[3, k])

    ship = pltpu.make_async_remote_copy(
        src_ref=tab,
        dst_ref=other,
        send_sem=w_sem.at[0],
        recv_sem=w_sem.at[1],
        device_id=partner,
        device_id_type=MESH,
    )

    def send_result(k):
        for copy in results(k):
            copy.start()

    place_line()
    send_z(0)
    pass_line(0, 0)
    pass_line(1, 0)
    loads[2].wait()
    prepare(0, count)
    for s in range(1, NZ + LAG3 + LAGP + 1):
        if s < NZ:
            pass_line(0, s)
        if 0 <= s - LAG3 < NZ:
            pass_plane(0, s - LAG3)
        if s == 5:
            send_z(1)
        if 8 <= s < 12:
            pass_line(1, s - 7)
        done = s - LAG3 - LAGP
        if 0 <= done < NZ:
            wait_plane(0, done)
            tile_dot(0, done)
        if 0 <= done - 1:
            tile_soft(0, done - 1)

    send_stats(0, 0)
    send_stats(0, 1)
    loads[1].wait()
    place, group, inner = reseeding(0)
    for s in range(5, NZ):
        pass_line(1, s)
    for s in range(4):
        pass_plane(1, s)
    spread_stats(0)
    for s in range(4, NZ):
        pass_plane(1, s)
    picked = picked_row(0, group, inner)
    for h in range(2):
        update(0, h, take_stats(0, h), picked, place, lambda k: prepare(*PARTS[k]))

    for s in range(NZ):
        wait_plane(1, s)
    ship.start()
    for t in range(NZ + 1):
        if t < NZ:
            tile_dot(1, t, t)
        if t:
            tile_soft(1, t - 1, t - 1)
        if t == NZ // 2:
            send_stats(1, 0)
    send_stats(1, 1)
    place, group, inner = reseeding(1)
    picked = picked_row(1, group, inner)
    for d, h in firsts:
        first_copy(d, h).wait_send()
    for i in range(ITERS):
        finish_sends(i)
    finish_stats(0)
    write_energy(0)
    spread_stats(1)
    ship.wait()
    for h in range(2):
        update(1, h, take_stats(1, h), picked, place, send_result)

    write_energy(1)
    their_place = place + (2 * g - 1) * count
    for k, (at, size) in enumerate(PARTS):
        keep, give = results(k)
        give.wait_recv()
        rows_k = slice(at, at + size)
        spot = lax.broadcasted_iota(jnp.int32, (size, D), 0) + at
        table = other[rows_k, :] + theirs[rows_k, :].astype(jnp.float32)
        other[rows_k, :] = jnp.where(spot == their_place, picked, table)
        put(k).start()
    finish_stats(1)
    for k in range(len(PARTS)):
        keep, give = results(k)
        keep.wait()
        give.wait_send()
        put(k).wait()


def shards(codebook, batch, dead_ids, reseed_rows, source_group):
    ids = jnp.concatenate([dead_ids, reseed_rows, source_group], axis=0)
    held = codebook.shape[0]
    count = held // 2
    anywhere = pl.BlockSpec(memory_space=pl.ANY)
    rows = NZ * NX * NY * 16
    dma = pltpu.SemaphoreType.DMA
    vmem = pltpu.VMEM
    table, energies = pl.pallas_call(
        kernel,
        out_shape=(
            jax.ShapeDtypeStruct((held, D), jnp.float32),
            jax.ShapeDtypeStruct((ITERS, 1, 8), jnp.float32),
        ),
        in_specs=[pl.BlockSpec(memory_space=pltpu.HBM)] * 3,
        out_specs=(anywhere, pl.BlockSpec(memory_space=vmem)),
        scratch_shapes=[
            vmem((NZ, NX, NY, 16, D), jnp.bfloat16),
            vmem((NZ, NX, NY, 16, D), jnp.bfloat16),
            vmem(batch.shape, batch.dtype),
            pltpu.SMEM(ids.shape, ids.dtype),
            vmem((16, D), jnp.bfloat16),
            vmem((NS, 2, 16, HALF), jnp.bfloat16),
            vmem((count, D), jnp.float32),
            vmem((count, D), jnp.bfloat16),
            vmem((count, LANES), jnp.float32),
            vmem((count, 2 * LANES), jnp.float32),
            vmem((count, 2 * LANES), jnp.float32),
            vmem((2 * NZ, count, LANES), jnp.float32),
            vmem((count, rows), jnp.bfloat16),
            vmem((count, D), jnp.float32),
            vmem((count, LANES), jnp.float32),
            vmem((count, D), jnp.float32),
            vmem((count, D), jnp.bfloat16),
            vmem((count, D), jnp.bfloat16),
            vmem((2 * NZ, LANES), jnp.float32),
            vmem((ITERS, 2 * NZ, LANES), jnp.float32),
            vmem((ITERS, 2 * NZ, LANES), jnp.float32),
            vmem((ITERS, 8, LANES), jnp.float32),
            vmem((ITERS, NZ, 2, 8, LANES), jnp.float32),
            vmem((ITERS, NX, NY, 2, 8, LANES), jnp.float32),
            dma((3,)),
            dma((2, NS, 2)),
            dma((2, ITERS, NZ)),
            dma((2, ITERS, NZ, NS)),
            dma((2, ITERS, NZ)),
            dma((2, ITERS, NZ, 2)),
            dma((2, ITERS, NX, NY, 2)),
            dma((4, len(PARTS))),
            dma((2,)),
        ],
        compiler_params=pltpu.CompilerParams(
            collective_id=0, has_side_effects=True, vmem_limit_bytes=48 * 2**20
        ),
        name="soft_kmeans",
    )(codebook, batch, ids)
    return (table, energies)


def solution(mesh):
    return jax.shard_map(
        shards,
        mesh=mesh,
        in_specs=(P("cent", None), P(None, "rows", "cent", None), P(), P(), P()),
        out_specs=(P("cent", None), P(None, "rows", "cent")),
        check_vma=False,
    )
```
